256 devices in a mesh: ctx: 32 (over y, z), head: 8 (over x, core).
Axes of the slice: x: 4, y: 4, z: 8, core: 2. Of those that a mesh axis runs over, the one named last changes fastest.
Arguments:
- latent_cache: bfloat16 [1024, 64, 576], P('ctx'), may hold values from -9 to 9
- queries: bfloat16 [4096, 128, 576], P('ctx', 'head'), may hold values from -16 to 16
- selected: int32 [4096, 8], P('ctx'), may hold values from 0 to 1023, as said below
- block_home: int32 [1024], replicated, may hold values from 0 to 1023, as said below
- w_uv: bfloat16 [128, 512, 128], P('head'), may hold values from -0.25 to 0.25
- out_grad: bfloat16 [4096, 128, 128], P('ctx', 'head'), may hold values from -6 to 6
Outputs:
- head_out: bfloat16 [4096, 128, 128], P('ctx', 'head')
- query_grad: bfloat16 [4096, 128, 576], P('ctx', 'head')
- cache_grad: bfloat16 [1024, 64, 576], P('ctx', 'head')
- weight_grad: bfloat16 [128, 512, 128], P('head', 'ctx')
The draws below stay inside these ranges and needn't reach their ends.
Inputs may be any that keep to these rules, and one draw needn't show every extreme that they name: `selected`: each row names 8 different blocks; the 128 queries of one ctx index together name exactly 16 different blocks, of which at most 2 are stored on one ctx index (the one holding row block_home[b]), and exactly 2 on at least one. `block_home`: each stored row holds exactly one block.
All inputs are finite; a program needn't handle non-finite values.
Results may differ from the reference program's by a relative error of at most 0.0057.
Values may be sent and summed in bfloat16 or wider, within the bound.
No kernel may reach another device: no remote copies, remote signals or barrier semaphores. Data moves between devices by JAX's collectives and lax.ppermute only.
A program may use at most 128 MiB of HBM per device.

```python
import jax
import jax.numpy as jnp
from jax import lax

HEADS = 128
KL = 512
VD = 128
KV = 576
BT = 64
TOPK = 8
UNIQ = 16
CAP = 2
Q_DEV = 128
BLK_DEV = 32
QUERIES = 4096
N_CTX = 32


def cache_base(key):
    return jax.random.fold_in(key, 101)


def token_key(base, stored, token):
    return jax.random.fold_in(jax.random.fold_in(base, stored), token)


def block_plan(key):
    total = BLK_DEV * N_CTX
    home = jax.random.permutation(jax.random.fold_in(key, 201), total).astype(jnp.int32)
    inverse = jnp.argsort(home).astype(jnp.int32)
    full = max(UNIQ // (2 * CAP), (UNIQ - N_CTX + CAP - 2) // (CAP - 1))
    single = UNIQ - full * CAP
    hotness = jax.random.randint(jax.random.fold_in(key, 202), (N_CTX,), 0, 4) * 4096
    owner_draw = jax.random.randint(jax.random.fold_in(key, 203), (N_CTX, N_CTX), 0, 4096) + hotness[None, :]
    ranked = owner_draw * N_CTX + jnp.arange(N_CTX)[None, :]
    order = jnp.argsort(-ranked, axis=1).astype(jnp.int32)
    slot_draw = jax.random.randint(jax.random.fold_in(key, 204), (N_CTX, N_CTX, BLK_DEV), 0, 65536)
    slot_draw = slot_draw * BLK_DEV + jnp.arange(BLK_DEV)[None, None, :]
    slot_order = jnp.argsort(slot_draw, axis=2)[:, :, :CAP].astype(jnp.int32)
    full_own = order[:, :full]
    full_slots = jnp.take_along_axis(slot_order, full_own[:, :, None], axis=1)
    full_rows = (full_own[:, :, None] * BLK_DEV + full_slots).reshape(N_CTX, full * CAP)
    one_own = order[:, full:full + single]
    one_slots = jnp.take_along_axis(slot_order[:, :, 0], one_own, axis=1)
    one_rows = one_own * BLK_DEV + one_slots
    pool_rows = jnp.concatenate([full_rows, one_rows], axis=1)
    pool_blocks = inverse[pool_rows]
    picking = jax.random.randint(jax.random.fold_in(key, 205), (N_CTX, Q_DEV, UNIQ), 0, 65536)
    picking = picking * UNIQ + jnp.arange(UNIQ)[None, None, :]
    pivot = (jnp.arange(Q_DEV) % UNIQ)[None, :, None] == jnp.arange(UNIQ)[None, None, :]
    picking = jnp.where(pivot, 1 << 30, picking)
    top_index = lax.top_k(picking, TOPK)[1]
    spread_pool = jnp.broadcast_to(pool_blocks[:, None, :], (N_CTX, Q_DEV, UNIQ))
    chosen = jnp.take_along_axis(spread_pool, top_index, axis=2)
    return (home, chosen.reshape(N_CTX * Q_DEV, TOPK).astype(jnp.int32))


def draw_block_home(key, part):
    return block_plan(key)[0]


def draw_selected(key, part):
    return block_plan(key)[1]


def draw_latent_cache(key, part):
    base = cache_base(key)
    stored = jnp.arange(BLK_DEV * N_CTX)
    tokens = jnp.arange(BT)

    def one_row(row, token):
        return jax.random.normal(token_key(base, row, token), (KV,), jnp.float32)
    rows = jax.vmap(jax.vmap(one_row, (None, 0)), (0, None))(stored, tokens)
    return jnp.clip(rows, -6.0, 6.0).astype(jnp.bfloat16)


def draw_queries(key, part):
    key = jax.random.fold_in(key, 4)
    result = jax.random.normal(key, (QUERIES, HEADS, KV), jnp.float32)
    return jnp.clip(result, -6.0, 6.0).astype(jnp.bfloat16)


def shard_levels(rng, dims, cuts, least, high):
    factor_of, own = 1.0, jax.random.fold_in(rng, 6)
    for axis_at, parts in cuts:
        steps = jnp.exp(jax.random.uniform(jax.random.fold_in(own, axis_at), (parts,), jnp.float32, least / len(cuts), high / len(cuts)))
        factor_of = factor_of * jnp.repeat(steps, dims[axis_at] // parts).reshape([-1 if axis == axis_at else 1 for axis in range(len(dims))])
    return factor_of


def normal_values(rng, extent, width, most, shards=(), kind=jnp.bfloat16):
    array = width * jax.random.normal(rng, extent, jnp.float32)
    if shards:
        array = array * shard_levels(rng, extent, shards, -0.22, 0.18)
    return jnp.clip(array, -most, most).astype(kind)


def setup_inputs(seed: int = 0) -> dict:
    key_of = jax.random.split(jax.random.key(seed), 7)
    latent_cache = draw_latent_cache(jax.random.fold_in(key_of[6], 71), 0)
    queries = draw_queries(jax.random.fold_in(key_of[6], 71), 0)
    selected = draw_selected(jax.random.fold_in(key_of[6], 71), 0)
    block_home = draw_block_home(jax.random.fold_in(key_of[6], 71), 0)
    w_uv = normal_values(key_of[4], (HEADS, KL, VD), KL ** -0.5, 0.25, ((0, 8),))
    out_grad = normal_values(key_of[5], (QUERIES, HEADS, VD), 1.0, 6.0, ((0, 32), (1, 8)))
    return dict(latent_cache=latent_cache, queries=queries, selected=selected, block_home=block_home, w_uv=w_uv, out_grad=out_grad)


softmax_scale = 192.0 ** -0.5
group_rows = 16


def reference(latent_cache, queries, selected, block_home, w_uv, out_grad):
    feature = latent_cache.shape[2]
    latent = w_uv.shape[1]
    groups = queries.shape[0] // group_rows
    stored = block_home[selected].astype(jnp.int32)
    q_blocks = queries.reshape(groups, group_rows, queries.shape[1], feature)
    r_blocks = stored.reshape(groups, group_rows, selected.shape[1])
    d_blocks = out_grad.reshape(groups, group_rows, out_grad.shape[1], out_grad.shape[2])
    weights = w_uv.astype(jnp.float32)

    def block_step(totals, inputs):
        grad_cache, grad_weight = totals
        q_part, r_part, d_part = inputs
        key_rows = latent_cache[r_part].reshape(group_rows, -1, feature).astype(jnp.float32)
        values = key_rows[:, :, :latent]
        q_float = q_part.astype(jnp.float32)
        scores = jnp.einsum("ghc,gjc->ghj", q_float, key_rows) * softmax_scale
        row_max = jnp.max(scores, axis=-1, keepdims=True)
        powers = jnp.exp(scores - row_max)
        attend = powers / jnp.sum(powers, axis=-1, keepdims=True)
        attend_low = lax.optimization_barrier(attend.astype(jnp.bfloat16)).astype(jnp.float32)
        latent_out = jnp.einsum("ghj,gjc->ghc", attend_low, values).astype(jnp.bfloat16)
        lat_float = lax.optimization_barrier(latent_out).astype(jnp.float32)
        head_out = jnp.einsum("ghc,hcv->ghv", lat_float, weights).astype(jnp.bfloat16)
        d_float = d_part.astype(jnp.float32)
        d_latent = jnp.einsum("ghv,hcv->ghc", d_float, weights).astype(jnp.bfloat16)
        dlat_float = lax.optimization_barrier(d_latent).astype(jnp.float32)
        grad_weight = grad_weight + jnp.einsum("ghc,ghv->hcv", lat_float, d_float)
        d_attend = jnp.einsum("ghc,gjc->ghj", dlat_float, values)
        inner_sum = jnp.sum(attend * d_attend, axis=-1, keepdims=True)
        d_scores = (attend * (d_attend - inner_sum) * softmax_scale).astype(jnp.bfloat16)
        ds_float = lax.optimization_barrier(d_scores).astype(jnp.float32)
        d_query = jnp.einsum("ghj,gjc->ghc", ds_float, key_rows).astype(jnp.bfloat16)
        d_keys = jnp.einsum("ghj,ghc->gjc", ds_float, q_float)
        d_values = jnp.einsum("ghj,ghc->gjc", attend_low, dlat_float)
        d_keys = d_keys.at[:, :, :latent].add(d_values)
        update = d_keys.reshape(group_rows, r_part.shape[1], latent_cache.shape[1], feature)
        grad_cache = grad_cache.at[r_part].add(update)
        return (grad_cache, grad_weight), (head_out, d_query)

    start_sum = (jnp.zeros(latent_cache.shape, jnp.float32), jnp.zeros(w_uv.shape, jnp.float32))
    (grad_cache, grad_weight), (outputs, d_queries) = lax.scan(block_step, start_sum, (q_blocks, r_blocks, d_blocks))
    return (outputs.reshape(out_grad.shape), d_queries.reshape(queries.shape),
            grad_cache.astype(jnp.bfloat16), grad_weight.astype(jnp.bfloat16))
```

```python
import functools

import jax
import jax.numpy as jnp
from jax import lax
from jax.experimental import pallas as pl
from jax.experimental.pallas import tpu as pltpu
from jax.sharding import PartitionSpec as P

NY, NZ, NX, NC = 4, 8, 4, 2
UNIQ = 16
CAP = 2
OUTSIDE = -1.0e6
TILE = 4

softmax_scale = 192.0 ** (-0.5)

BF = jnp.bfloat16
F32 = jnp.float32


def dot(a, b, ca, cb):
    return lax.dot_general(a, b, (((ca,), (cb,)), ((), ())), preferred_element_type=F32)


def attend_kernel(
    y_ref, k0_ref, k1_ref, k2_ref, k3_ref, kc_ref, q_ref, dl_ref, og_ref, w_ref,
    dq_ref, ho_ref, keep_ref, send_ref, pool_ref, keys,
):
    step = pl.program_id(0)
    tile, nq, wide = q_ref.shape
    feature = dq_ref.shape[2]
    latent = dl_ref.shape[2]
    rows = keys.shape[0]
    part = k0_ref.shape[0]
    group = part // UNIQ
    half = pl.num_programs(0) // 2

    @pl.when(step == 0)
    def _():
        for at, ref in enumerate((k0_ref, k1_ref, k2_ref, k3_ref)):
            keys[at * part:(at + 1) * part, :feature] = ref[...]
        keys[NX * part:, :feature] = kc_ref[...]
        owner = (lax.broadcasted_iota(jnp.int32, (rows, wide - feature), 0) // group) % UNIQ
        lane = lax.broadcasted_iota(jnp.int32, (rows, wide - feature), 1)
        keys[:, feature:] = (owner == lane).astype(F32).astype(BF)
        pool_ref[...] = jnp.zeros_like(pool_ref)

    ka = keys[...]
    values = ka[:, :latent]
    q = q_ref[...].reshape(tile * nq, wide)
    dl = dl_ref[...].reshape(tile * nq, latent)
    s = dot(q, ka, 1, 1)
    top = jnp.max(s, axis=1, keepdims=True)
    p = jnp.exp((s - top) * softmax_scale)
    a = p * (1.0 / jnp.sum(p, axis=1, keepdims=True))
    low = a.astype(BF)
    out = dot(low, values, 1, 0).astype(BF)
    da = dot(dl, values, 1, 1)
    inner = jnp.sum(a * da, axis=1, keepdims=True)
    ds = (a * (da - inner) * softmax_scale).astype(BF)
    dq = dot(ds, ka, 1, 0)
    dq_ref[...] = dq[:, :feature].astype(BF).reshape(tile, nq, feature)
    pool_ref[:, latent:] += dot(ds, q[:, latent:feature], 0, 0)
    pool_ref[:, :latent] += dot(ds, q[:, :latent], 0, 0) + dot(low, dl, 0, 0)
    y = y_ref[0]
    for t in range(tile):
        o = out[t * nq:(t + 1) * nq]
        ho_ref[t] = dot(o, w_ref[t], 1, 0).astype(BF)
        wt = dot(o, og_ref[t], 0, 0)
        wt = wt.reshape(NY, NZ, latent // (NY * NZ), wt.shape[1])
        for part_y in range(NY):
            rel = part_y ^ y
            piece = wt[part_y]
            slot = jnp.where(rel == 0, 0, 1)
            kept = (rel == 0) | (rel == jnp.where(step < half, 3, 1))

            @pl.when(kept)
            def _():
                keep_ref[0, slot, :, t] = piece

            @pl.when(jnp.logical_not(kept))
            def _():
                send_ref[0, jnp.where(rel == 2, 1, 0), :, t] = piece.astype(BF)


def attend(y, parts, other, q, dl, og, w):
    heads, nq, wide = q.shape
    latent = dl.shape[2]
    vd = og.shape[2]
    part, feature = other.shape[0] // NX, other.shape[1]
    rows = 2 * NX * part
    tile = TILE
    steps = heads // tile
    per = steps // 2
    sub = latent // (NY * NZ)
    whole = lambda shape: pl.BlockSpec(shape, lambda i: (0,) * len(shape))
    heads_of = lambda *shape: pl.BlockSpec((tile,) + shape, lambda i: (i, 0, 0))
    split = pl.BlockSpec((1, 2, NZ, tile, sub, vd), lambda i: (i // per, 0, 0, i % per, 0, 0))
    flops = 2 * heads * nq * rows * (3 * feature + 3 * latent)
    return pl.pallas_call(
        attend_kernel,
        grid=(steps,),
        in_specs=[pl.BlockSpec(memory_space=pltpu.SMEM)]
        + [whole((part, feature))] * NX
        + [whole((NX * part, feature)), heads_of(nq, wide), heads_of(nq, latent),
           heads_of(nq, vd), heads_of(latent, vd)],
        out_specs=[heads_of(nq, feature), heads_of(nq, vd), split, split, whole((rows, feature))],
        out_shape=[
            jax.ShapeDtypeStruct((heads, nq, feature), BF),
            jax.ShapeDtypeStruct((heads, nq, vd), BF),
            jax.ShapeDtypeStruct((2, 2, NZ, heads // 2, sub, vd), F32),
            jax.ShapeDtypeStruct((2, 2, NZ, heads // 2, sub, vd), BF),
            jax.ShapeDtypeStruct((rows, feature), F32),
        ],
        scratch_shapes=[pltpu.VMEM((rows, wide), BF)],
        compiler_params=pltpu.CompilerParams(vmem_limit_bytes=56 * 1024 * 1024),
        cost_estimate=pl.CostEstimate(
            flops=flops, bytes_accessed=20_000_000, transcendentals=heads * nq * rows
        ),
    )(y, *parts, other, q, dl, og, w)


def by_ctx(move):
    return [(y * NZ + z, move(y) * NZ + z) for y in range(NY) for z in range(NZ)]


def by_head(move):
    return [(x * NC + c, move(x, c)) for x in range(NX) for c in range(NC)]


def to_x(k):
    return by_head(lambda x, c: (x + k) % NX * NC + c)


def from_x(k):
    return by_head(lambda x, c: (x - k) % NX * NC + c)


OTHER_CORE = by_head(lambda x, c: x * NC + 1 - c)


def body(latent_cache, queries, selected, block_home, w_uv, out_grad):
    owners = NY * NZ
    blk_dev, block_len, feature = latent_cache.shape
    latent = w_uv.shape[1]
    total = block_home.shape[0]
    nq, heads, _ = queries.shape
    share = block_len // (NX * NC)
    head_at = lax.axis_index("head")
    y_at = lax.axis_index("ctx") // NZ

    flat = selected.reshape(-1)
    flat_home = jnp.sum(
        jnp.where(flat[:, None] == jnp.arange(total)[None, :], block_home[None, :], 0), axis=1
    )
    slots = jnp.arange(blk_dev, dtype=jnp.int32)[None, :]
    stored = jnp.arange(total, dtype=jnp.int32).reshape(owners, blk_dev)
    present = jnp.max(
        (flat_home[:, None, None] == stored[None]).astype(jnp.int32), axis=0
    )
    first = jnp.min(jnp.where(present > 0, slots, blk_dev), axis=1)
    last = jnp.max(jnp.where(present > 0, slots, -1), axis=1)
    request = jnp.stack(
        [jnp.where(first < blk_dev, first, -1), jnp.where(last > first, last, -1)], axis=1
    )
    asked = lax.all_to_all(request, "ctx", split_axis=0, concat_axis=0, tiled=True)

    mine = lax.dynamic_slice_in_dim(latent_cache, head_at * share, share, axis=1)
    outgoing = mine[jnp.maximum(asked.reshape(-1), 0)]
    arrived = lax.all_to_all(
        outgoing.reshape(owners, CAP, share, feature), "ctx", split_axis=0, concat_axis=0, tiled=True
    ).reshape(owners * CAP, share, feature)

    valid = (request >= 0).reshape(-1)
    count = jnp.arange(owners * CAP)
    place = jnp.sum((valid[None, :] & (count[None, :] < count[:, None])).astype(jnp.int32), axis=1)
    hit = valid[None, :] & (place[None, :] == jnp.arange(UNIQ)[:, None])
    source = jnp.sum(jnp.where(hit, count[None, :], 0), axis=1)
    slot_home = (jnp.arange(owners)[:, None] * blk_dev + jnp.maximum(request, 0)).reshape(-1)
    pool_home = jnp.sum(jnp.where(hit, slot_home[None, :], 0), axis=1)
    chosen = jnp.max(
        (flat_home.reshape(nq, -1)[:, :, None] == pool_home[None, None, :]).astype(jnp.int32), axis=1
    )

    wide = (feature + UNIQ + 127) // 128 * 128
    bias = jnp.where(chosen > 0, 0.0, OUTSIDE).astype(BF)
    q_heads = jnp.concatenate(
        [
            jnp.swapaxes(queries, 0, 1),
            jnp.broadcast_to(bias[None], (heads, nq, UNIQ)),
            jnp.zeros((heads, nq, wide - feature - UNIQ), BF),
        ],
        axis=2,
    )
    og_heads = jnp.swapaxes(out_grad, 0, 1)
    d_latent = jnp.einsum(
        "hqv,hcv->hqc", og_heads, w_uv, preferred_element_type=F32
    ).astype(BF)

    own = arrived[source].reshape(UNIQ * share, feature)
    parts = [own] + [lax.ppermute(own, "head", from_x(k)) for k in range(1, NX)]
    near = jnp.concatenate(parts, axis=0)
    other = lax.ppermute(near, "head", OTHER_CORE)

    d_query, out_heads, keep, send, pool = attend(
        y_at.astype(jnp.int32).reshape(1), parts, other, q_heads, d_latent, og_heads, w_uv
    )

    near_rows = NX * UNIQ * share
    pair = pool[:near_rows] + lax.ppermute(pool[near_rows:], "head", OTHER_CORE)
    pair = pair.reshape(NX, UNIQ * share, feature)
    summed = pair[0]
    for k in range(1, NX):
        summed = summed + lax.ppermute(pair[k].astype(BF), "head", to_x(k)).astype(F32)
    summed = summed.astype(BF).reshape(UNIQ, share, feature)
    outbound = summed[jnp.minimum(place, UNIQ - 1)]
    returned = lax.all_to_all(
        outbound.reshape(owners, CAP, share, feature), "ctx", split_axis=0, concat_axis=0, tiled=True
    ).reshape(owners * CAP, share, feature)
    slot_hot = (jnp.arange(blk_dev)[:, None] == asked.reshape(-1)[None, :]).astype(BF)
    cache_grad = jnp.einsum(
        "sr,rtc->stc", slot_hot, returned, preferred_element_type=F32
    ).astype(BF)

    toward = (by_ctx(lambda y: y ^ 1), by_ctx(lambda y: y ^ 3))
    halves = []
    for at in range(2):
        halves.append(keep[at] + lax.ppermute(send[at], "ctx", toward[at]).astype(F32))
    done = []
    for at in range(2):
        back = lax.ppermute(halves[at][1].astype(BF), "ctx", toward[1 - at])
        done.append(halves[at][0] + back.astype(F32))
    column = jnp.concatenate(done, axis=1).astype(BF)
    groups = [[y * NZ + z for z in range(NZ)] for y in range(NY)]
    spread = lax.all_to_all(
        column, "ctx", split_axis=0, concat_axis=0, tiled=True, axis_index_groups=groups
    )
    weight_grad = jnp.sum(spread.astype(F32), axis=0).astype(BF)

    return (
        jnp.swapaxes(out_heads, 0, 1),
        jnp.swapaxes(d_query, 0, 1),
        cache_grad,
        weight_grad,
    )


def solution(mesh):
    in_specs = (
        P("ctx", None, None),
        P("ctx", "head", None),
        P("ctx", None),
        P(),
        P("head", None, None),
        P("ctx", "head", None),
    )
    out_specs = (
        P("ctx", "head", None),
        P("ctx", "head", None),
        P("ctx", "head", None),
        P("head", "ctx", None),
    )
    return jax.shard_map(body, mesh=mesh, in_specs=in_specs, out_specs=out_specs, check_vma=False)
```

```python
import jax
import jax.numpy as jnp
from jax import lax
from jax.experimental import pallas as pl
from jax.experimental.pallas import tpu as pltpu
from jax.sharding import PartitionSpec as P

NY, NZ, NX, NC = 4, 8, 4, 2
UNIQ = 16
CAP = 2
OUTSIDE = -1.0e6
TILE = 4
SUB = 2
CHUNK = 256
VMEM_LIMIT = 32 * 1024 * 1024

softmax_scale = 192.0 ** (-0.5)
LOG2E = 1.4426950408889634

BF = jnp.bfloat16
F32 = jnp.float32


def dot(a, b, ca, cb):
    return lax.dot_general(a, b, (((ca,), (cb,)), ((), ())), preferred_element_type=F32)


def forward_kernel(
    y_ref, k0_ref, k1_ref, k2_ref, k3_ref, kc_ref, bias_ref, qt_ref, dlt_ref, og_ref,
    low_ref, ds_ref, out_ref, keys_ref, own_a_ref, next_a_ref, send_a_ref,
    own_b_ref, next_b_ref, send_b_ref, values_t, pieces,
):
    step = pl.program_id(0)
    tile, nq, _ = og_ref.shape
    wide = keys_ref.shape[1]
    rows, feature = keys_ref.shape[0], k0_ref.shape[1]
    latent = dlt_ref.shape[1]
    part = k0_ref.shape[0]
    group = part // UNIQ
    half = pl.num_programs(0) // 2

    @pl.when(step == 0)
    def _():
        for at, ref in enumerate((k0_ref, k1_ref, k2_ref, k3_ref)):
            keys_ref[at * part:(at + 1) * part, :feature] = ref[...]
        keys_ref[NX * part:, :feature] = kc_ref[:, :feature]
        owner = (lax.broadcasted_iota(jnp.int32, (rows, wide - feature), 0) // group) % UNIQ
        lane = lax.broadcasted_iota(jnp.int32, (rows, wide - feature), 1)
        keys_ref[:, feature:] = (owner == lane).astype(F32).astype(BF)
        values_t[...] = keys_ref[:, :latent].T

    per = min(SUB, tile)
    sub = per * nq
    rest = jnp.zeros((wide - feature - UNIQ, sub), BF)
    bias = jnp.concatenate([bias_ref[...]] * per, axis=1)

    def scored(j):
        q = jnp.concatenate([qt_ref[j * per + t] for t in range(per)], axis=1)
        return jnp.concatenate([q, bias, rest], axis=0)

    def carried(j):
        return jnp.concatenate([dlt_ref[j * per + t] for t in range(per)], axis=1)

    cols = [slice(at, at + sub) for at in range(0, tile * nq, sub)]
    rate = softmax_scale * LOG2E
    outs = []
    chunks = [slice(k, k + CHUNK) for k in range(0, rows, CHUNK)]
    def top_of(s):
        t = s[0].max(axis=0, keepdims=True)
        for x in s[1:]:
            t = jnp.maximum(t, x.max(axis=0, keepdims=True))
        return t * rate
    n = len(cols)
    ss, dd, pp = [None] * n, [None] * n, [None] * n
    for j in range(n + 1):
        if j < n:
            ss[j], dd[j] = [], []
            q, dl = scored(j), carried(j)
        if j > 0:
            pp[j - 1], total, inner = [], 0.0, 0.0
            top = top_of(ss[j - 1])
        for ki, k in enumerate(chunks):
            if j < n:
                ss[j].append(dot(keys_ref[k], q, 1, 0))
            if j > 0:
                p = jnp.exp2(ss[j - 1][ki] * rate - top)
                pp[j - 1].append(p)
                total = total + p.sum(axis=0, keepdims=True)
                inner = inner + (p * dd[j - 1][ki]).sum(axis=0, keepdims=True)
        if j > 0:
            inv = 1.0 / total
            inner = inner * inv
            scaled = inv * softmax_scale
        for ki, k in enumerate(chunks):
            if j < n:
                dd[j].append(dot(keys_ref[k, :latent], dl, 1, 0))
            if j > 0:
                p = pp[j - 1][ki]
                low_ref[k, cols[j - 1]] = (p * inv).astype(BF)
                ds_ref[k, cols[j - 1]] = (p * scaled * (dd[j - 1][ki] - inner)).astype(BF)
        if j > 0:
            out = dot(values_t[...], low_ref[:, cols[j - 1]], 1, 0).astype(BF)
            for t in range(per):
                out_ref[(j - 1) * per + t] = out[:, t * nq:(t + 1) * nq]
            outs.append(out)
    y = y_ref[0]
    for t in range(tile):
        at = t * nq % sub
        wt = dot(outs[t * nq // sub][:, at:at + nq], og_ref[t], 1, 0)
        wt = wt.reshape(NY, NZ, latent // (NY * NZ), wt.shape[1])
        for part_y in range(NY):
            pieces[part_y ^ y, :, t] = wt[part_y]

    @pl.when(step < half)
    def _():
        own_a_ref[...] = pieces[0]
        next_a_ref[...] = pieces[3]
        send_a_ref[0] = pieces[1].astype(BF)
        send_a_ref[1] = pieces[2].astype(BF)

    @pl.when(step >= half)
    def _():
        own_b_ref[...] = pieces[0]
        next_b_ref[...] = pieces[1]
        send_b_ref[0] = pieces[3].astype(BF)
        send_b_ref[1] = pieces[2].astype(BF)


def forward(y, parts, other, bias, qt, dlt, og):
    heads, nq, vd = og.shape
    wide, latent = other.shape[1], dlt.shape[1]
    part, feature = parts[0].shape
    rows = 2 * NX * part
    tile = TILE
    steps = heads // tile
    per = steps // 2
    sub = latent // (NY * NZ)
    whole = lambda *shape: pl.BlockSpec(shape, lambda i: (0,) * len(shape))
    cols = lambda n: pl.BlockSpec((n, tile * nq), lambda i: (0, i))
    heads_of = lambda *shape: pl.BlockSpec((tile,) + shape, lambda i: (i, 0, 0))
    at_a = lambda i: jnp.minimum(i, per - 1)
    at_b = lambda i: jnp.maximum(i - per, 0)

    def pieces_at(at):
        one = pl.BlockSpec((NZ, tile, sub, vd), lambda i: (0, at(i), 0, 0))
        two = pl.BlockSpec((2, NZ, tile, sub, vd), lambda i: (0, 0, at(i), 0, 0))
        return [one, one, two]

    shape = jax.ShapeDtypeStruct
    piece_shapes = [
        shape((NZ, heads // 2, sub, vd), F32), shape((NZ, heads // 2, sub, vd), F32),
        shape((2, NZ, heads // 2, sub, vd), BF),
    ]
    return pl.pallas_call(
        forward_kernel,
        grid=(steps,),
        in_specs=[pl.BlockSpec(memory_space=pltpu.SMEM)]
        + [whole(part, feature)] * NX
        + [whole(NX * part, wide), whole(UNIQ, nq), heads_of(feature, nq), heads_of(latent, nq),
           heads_of(nq, vd)],
        out_specs=[cols(rows), cols(rows), heads_of(latent, nq), whole(rows, wide)]
        + pieces_at(at_a) + pieces_at(at_b),
        out_shape=[
            shape((rows, heads * nq), BF), shape((rows, heads * nq), BF),
            shape((heads, latent, nq), BF), shape((rows, wide), BF),
        ] + piece_shapes * 2,
        scratch_shapes=[pltpu.VMEM((latent, rows), BF), pltpu.VMEM((NY, NZ, tile, sub, vd), F32)],
        compiler_params=pltpu.CompilerParams(vmem_limit_bytes=VMEM_LIMIT),
        cost_estimate=pl.CostEstimate(
            flops=2 * heads * nq * rows * (wide + 2 * latent), bytes_accessed=16_000_000,
            transcendentals=heads * nq * rows,
        ),
    )(y, *parts, other, bias, qt, dlt, og)


def pool_kernel(low_ref, ds_ref, qt_ref, dlt_ref, near_ref, far_ref):
    tile, latent, nq = dlt_ref.shape
    feature = near_ref.shape[1]
    rows = near_ref.shape[0]

    @pl.when(pl.program_id(0) == 0)
    def _():
        near_ref[...] = jnp.zeros_like(near_ref)
        far_ref[...] = jnp.zeros_like(far_ref)

    q = jnp.concatenate([qt_ref[t] for t in range(tile)], axis=1)
    dl = jnp.concatenate([dlt_ref[t] for t in range(tile)], axis=1)
    for at, ref in ((0, near_ref), (rows, far_ref)):
        ds = ds_ref[at:at + rows]
        low = low_ref[at:at + rows]
        ref[:, :latent] += dot(ds, q[:latent], 1, 1) + dot(low, dl, 1, 1)
        ref[:, latent:feature] += dot(ds, q[latent:], 1, 1)


def pool_grads(low, ds, qt, dlt, wide):
    rows = low.shape[0]
    heads, feature, nq = qt.shape
    latent = dlt.shape[1]
    tile = TILE
    cols = pl.BlockSpec((rows, tile * nq), lambda i: (0, i))
    heads_of = lambda *shape: pl.BlockSpec((tile,) + shape, lambda i: (i, 0, 0))
    out = lambda n: pl.BlockSpec((rows // 2, n), lambda i: (0, 0))
    return pl.pallas_call(
        pool_kernel,
        grid=(heads // tile,),
        in_specs=[cols, cols, heads_of(feature, nq), heads_of(latent, nq)],
        out_specs=[out(feature), out(wide)],
        out_shape=[jax.ShapeDtypeStruct((rows // 2, n), F32) for n in (feature, wide)],
        compiler_params=pltpu.CompilerParams(vmem_limit_bytes=VMEM_LIMIT),
        cost_estimate=pl.CostEstimate(
            flops=2 * heads * nq * rows * (feature + latent), bytes_accessed=12_000_000,
            transcendentals=0,
        ),
    )(low, ds, qt, dlt)


def rest_kernel(ds_ref, keys_ref, out_ref, w_ref, dq_ref, ho_ref):
    tile, feature, nq = dq_ref.shape
    dq = dot(keys_ref[...], ds_ref[...], 0, 0)[:feature].astype(BF)
    for t in range(tile):
        dq_ref[t] = dq[:, t * nq:(t + 1) * nq]
        ho_ref[t] = dot(out_ref[t], w_ref[t], 0, 0).astype(BF)


def rest(ds, keys, out, w, feature):
    heads, latent, vd = w.shape
    rows, wide = keys.shape
    nq = out.shape[2]
    tile = TILE
    heads_of = lambda *shape: pl.BlockSpec((tile,) + shape, lambda i: (i, 0, 0))
    return pl.pallas_call(
        rest_kernel,
        grid=(heads // tile,),
        in_specs=[pl.BlockSpec((rows, tile * nq), lambda i: (0, i)),
                  pl.BlockSpec((rows, wide), lambda i: (0, 0)), heads_of(latent, nq),
                  heads_of(latent, vd)],
        out_specs=[heads_of(feature, nq), heads_of(nq, vd)],
        out_shape=[jax.ShapeDtypeStruct((heads, feature, nq), BF),
                   jax.ShapeDtypeStruct((heads, nq, vd), BF)],
        compiler_params=pltpu.CompilerParams(vmem_limit_bytes=VMEM_LIMIT),
        cost_estimate=pl.CostEstimate(
            flops=2 * heads * nq * rows * feature, bytes_accessed=12_000_000, transcendentals=0
        ),
    )(ds, keys, out, w)


def settle_kernel(asked_ref, returned_ref, out_ref, total):
    total[...] = jnp.zeros_like(total)

    def add(at, carry):
        slot = asked_ref[at]

        @pl.when(slot >= 0)
        def _():
            total[slot] += returned_ref[at].astype(F32)

        return carry

    lax.fori_loop(0, returned_ref.shape[0], add, 0)
    out_ref[...] = total[...].astype(BF)


def settle(asked, returned, blk_dev):
    _, share, feature = returned.shape
    return pl.pallas_call(
        settle_kernel,
        in_specs=[pl.BlockSpec(memory_space=pltpu.SMEM), pl.BlockSpec(memory_space=pltpu.VMEM)],
        out_specs=pl.BlockSpec(memory_space=pltpu.VMEM),
        out_shape=jax.ShapeDtypeStruct((blk_dev, share, feature), BF),
        scratch_shapes=[pltpu.VMEM((blk_dev, share, feature), F32)],
        cost_estimate=pl.CostEstimate(flops=500_000, bytes_accessed=1_000_000, transcendentals=0),
    )(asked, returned)


def by_ctx(move):
    return [(y * NZ + z, move(y) * NZ + z) for y in range(NY) for z in range(NZ)]


def by_head(move):
    return [(x * NC + c, move(x, c)) for x in range(NX) for c in range(NC)]


def to_x(k):
    return by_head(lambda x, c: (x + k) % NX * NC + c)


def from_x(k):
    return by_head(lambda x, c: (x - k) % NX * NC + c)


OTHER_CORE = by_head(lambda x, c: x * NC + 1 - c)


def body(latent_cache, queries, selected, block_home, w_uv, out_grad):
    owners = NY * NZ
    blk_dev, block_len, feature = latent_cache.shape
    latent = w_uv.shape[1]
    total = block_home.shape[0]
    nq, heads, _ = queries.shape
    share = block_len // (NX * NC)
    head_at = lax.axis_index("head")
    y_at = lax.axis_index("ctx") // NZ

    flat = selected.reshape(-1)
    flat_home = jnp.sum(
        jnp.where(flat[:, None] == jnp.arange(total)[None, :], block_home[None, :], 0), axis=1
    )
    slots = jnp.arange(blk_dev, dtype=jnp.int32)[None, :]
    stored = jnp.arange(total, dtype=jnp.int32).reshape(owners, blk_dev)
    present = jnp.max(
        (flat_home[:, None, None] == stored[None]).astype(jnp.int32), axis=0
    )
    first = jnp.min(jnp.where(present > 0, slots, blk_dev), axis=1)
    last = jnp.max(jnp.where(present > 0, slots, -1), axis=1)
    request = jnp.stack(
        [jnp.where(first < blk_dev, first, -1), jnp.where(last > first, last, -1)], axis=1
    )
    asked = lax.all_to_all(request, "ctx", split_axis=0, concat_axis=0, tiled=True)

    q_t = jnp.transpose(queries, (1, 2, 0))
    og_heads = jnp.swapaxes(out_grad, 0, 1)
    mine = lax.dynamic_slice_in_dim(latent_cache, head_at * share, share, axis=1)
    asked, og_heads, mine = lax.optimization_barrier((asked, og_heads, mine))
    asked = asked.reshape(-1)

    outgoing = mine[jnp.maximum(asked, 0)]
    arrived = lax.all_to_all(
        outgoing.reshape(owners, CAP, share, feature), "ctx", split_axis=0, concat_axis=0, tiled=True
    ).reshape(owners * CAP, share, feature)

    valid = (request >= 0).reshape(-1)
    count = jnp.arange(owners * CAP)
    place = jnp.sum((valid[None, :] & (count[None, :] < count[:, None])).astype(jnp.int32), axis=1)
    hit = valid[None, :] & (place[None, :] == jnp.arange(UNIQ)[:, None])
    source = jnp.sum(jnp.where(hit, count[None, :], 0), axis=1)
    slot_home = (jnp.arange(owners)[:, None] * blk_dev + jnp.maximum(request, 0)).reshape(-1)
    pool_home = jnp.sum(jnp.where(hit, slot_home[None, :], 0), axis=1)
    chosen = jnp.max(
        (flat_home.reshape(nq, -1)[:, :, None] == pool_home[None, None, :]).astype(jnp.int32), axis=1
    )
    spot = jnp.minimum(place, UNIQ - 1)

    wide = (feature + UNIQ + 127) // 128 * 128
    bias = jnp.where(chosen > 0, 0.0, OUTSIDE).astype(BF).T
    d_latent = jnp.einsum(
        "hcv,hqv->hcq", w_uv, og_heads, preferred_element_type=F32
    ).astype(BF)
    arrived, bias, d_latent, source, spot = lax.optimization_barrier(
        (arrived, bias, d_latent, source, spot)
    )

    own = arrived[source].reshape(UNIQ * share, feature)
    parts = [own] + [lax.ppermute(own, "head", from_x(k)) for k in range(1, NX)]
    near_keys = jnp.pad(jnp.concatenate(parts, axis=0), ((0, 0), (0, wide - feature)))
    far_keys = lax.ppermute(near_keys, "head", OTHER_CORE)

    low, ds, out, keys, own_a, next_a, send_a, own_b, next_b, send_b = forward(
        y_at.astype(jnp.int32).reshape(1), parts, far_keys, bias, q_t, d_latent, og_heads
    )

    flip, turn = by_ctx(lambda y: y ^ 1), by_ctx(lambda y: y ^ 3)
    got_a = lax.ppermute(send_a, "ctx", flip)
    got_b = lax.ppermute(send_b, "ctx", turn)

    near, far = pool_grads(low, ds, q_t, d_latent, wide)
    far_in = lax.ppermute(far, "head", OTHER_CORE)
    got_a, got_b, _ = lax.optimization_barrier((got_a, got_b, far))
    pass_a = (next_a + got_a[1].astype(F32)).astype(BF)
    pass_b = (next_b + got_b[1].astype(F32)).astype(BF)
    last_a = lax.ppermute(pass_a, "ctx", turn)
    last_b = lax.ppermute(pass_b, "ctx", flip)

    near, far_in, _, _ = lax.optimization_barrier((near, far_in, pass_a, pass_b))
    size = UNIQ * share
    quarter = [near[k * size:(k + 1) * size] + far_in[k * size:(k + 1) * size, :feature] for k in range(NX)]
    ahead = {k: lax.ppermute(quarter[k].astype(BF), "head", to_x(k)) for k in (2, 1, 3)}
    summed = quarter[0]
    for k in range(1, NX):
        summed = summed + ahead[k].astype(F32)
    outbound = summed.astype(BF).reshape(UNIQ, share, feature)[spot]
    returned = lax.all_to_all(
        outbound.reshape(owners, CAP, share, feature), "ctx", split_axis=0, concat_axis=0, tiled=True
    ).reshape(owners * CAP, share, feature)

    last_a, last_b, _ = lax.optimization_barrier((last_a, last_b, outbound))
    column = jnp.concatenate(
        [
            own_a + got_a[0].astype(F32) + last_a.astype(F32),
            own_b + got_b[0].astype(F32) + last_b.astype(F32),
        ],
        axis=1,
    ).astype(BF)
    groups = [[y * NZ + z for z in range(NZ)] for y in range(NY)]
    spread = lax.all_to_all(
        column, "ctx", split_axis=0, concat_axis=0, tiled=True, axis_index_groups=groups
    )

    ds, out, _ = lax.optimization_barrier((ds, out, outbound))
    d_query, out_heads = rest(ds, keys, out, w_uv, feature)
    d_query, out_heads = jnp.transpose(d_query, (2, 0, 1)), jnp.swapaxes(out_heads, 0, 1)
    returned, spread, d_query, out_heads = lax.optimization_barrier(
        (returned, spread, d_query, out_heads)
    )

    cache_grad = settle(asked, returned, blk_dev)
    weight_grad = jnp.sum(spread.astype(F32), axis=0).astype(BF)
    return out_heads, d_query, cache_grad, weight_grad


def solution(mesh):
    in_specs = (
        P("ctx", None, None),
        P("ctx", "head", None),
        P("ctx", None),
        P(),
        P("head", None, None),
        P("ctx", "head", None),
    )
    out_specs = (
        P("ctx", "head", None),
        P("ctx", "head", None),
        P("ctx", "head", None),
        P("head", "ctx", None),
    )
    return jax.shard_map(body, mesh=mesh, in_specs=in_specs, out_specs=out_specs, check_vma=False)
```

```python
import jax
import jax.numpy as jnp
from jax import lax
from jax.experimental import pallas as pl
from jax.experimental.pallas import tpu as pltpu
from jax.sharding import PartitionSpec as P

NY, NZ, NX, NC = 4, 8, 4, 2
UNIQ = 16
CAP = 2
OUTSIDE = -1.0e6
TILE = 4
SUB = 2
CHUNK = 256
FORWARD_VMEM = 24 * 1024 * 1024
POOL_VMEM = 16 * 1024 * 1024
REST_VMEM = 56 * 1024 * 1024

softmax_scale = 192.0 ** (-0.5)
LOG2E = 1.4426950408889634

BF = jnp.bfloat16
F32 = jnp.float32


def dot(a, b, ca, cb):
    return lax.dot_general(a, b, (((ca,), (cb,)), ((), ())), preferred_element_type=F32)


def forward_kernel(
    at_ref, k0_ref, k1_ref, k2_ref, k3_ref, k4_ref, k5_ref, k6_ref, k7_ref, bias_ref, qt_ref,
    dlt_ref, og_ref, low_ref, ds_ref, out_ref, keys_ref, own_a_ref, next_a_ref, send_a_ref,
    own_b_ref, next_b_ref, send_b_ref, values_t, pieces,
):
    step = pl.program_id(0)
    tile, nq, _ = og_ref.shape
    wide = keys_ref.shape[1]
    rows, feature = keys_ref.shape[0], k0_ref.shape[1]
    latent = dlt_ref.shape[1]
    part = k0_ref.shape[0]
    group = part // UNIQ
    half = pl.num_programs(0) // 2

    @pl.when(step == 0)
    def _():
        for at, ref in enumerate((k0_ref, k1_ref, k2_ref, k3_ref, k4_ref, k5_ref, k6_ref, k7_ref)):
            keys_ref[at * part:(at + 1) * part, :feature] = ref[...]
        owner = (lax.broadcasted_iota(jnp.int32, (rows, wide - feature), 0) // group) % UNIQ
        lane = lax.broadcasted_iota(jnp.int32, (rows, wide - feature), 1)
        keys_ref[:, feature:] = (owner == lane).astype(F32).astype(BF)
        values_t[...] = keys_ref[:, :latent].T

    per = min(SUB, tile)
    sub = per * nq
    rest = jnp.zeros((wide - feature - UNIQ, sub), BF)
    bias = jnp.concatenate([bias_ref[...]] * per, axis=1)

    def scored(j):
        q = jnp.concatenate([qt_ref[j * per + t] for t in range(per)], axis=1)
        return jnp.concatenate([q, bias, rest], axis=0)

    def carried(j):
        return jnp.concatenate([dlt_ref[j * per + t] for t in range(per)], axis=1)

    cols = [slice(at, at + sub) for at in range(0, tile * nq, sub)]
    rate = softmax_scale * LOG2E
    outs = []
    chunks = [slice(k, k + CHUNK) for k in range(0, rows, CHUNK)]
    def top_of(s):
        t = s[0].max(axis=0, keepdims=True)
        for x in s[1:]:
            t = jnp.maximum(t, x.max(axis=0, keepdims=True))
        return t * rate
    n = len(cols)
    ss, dd, pp = [None] * n, [None] * n, [None] * n
    for j in range(n + 1):
        if j < n:
            ss[j], dd[j] = [], []
            q, dl = scored(j), carried(j)
        if j > 0:
            pp[j - 1], total, inner = [], 0.0, 0.0
            top = top_of(ss[j - 1])
        for ki, k in enumerate(chunks):
            if j < n:
                ss[j].append(dot(keys_ref[k], q, 1, 0))
            if j > 0:
                p = jnp.exp2(ss[j - 1][ki] * rate - top)
                pp[j - 1].append(p)
                total = total + p.sum(axis=0, keepdims=True)
                inner = inner + (p * dd[j - 1][ki]).sum(axis=0, keepdims=True)
        if j > 0:
            inv = 1.0 / total
            inner = inner * inv
            scaled = inv * softmax_scale
        for ki, k in enumerate(chunks):
            if j < n:
                dd[j].append(dot(keys_ref[k, :latent], dl, 1, 0))
            if j > 0:
                p = pp[j - 1][ki]
                low_ref[k, cols[j - 1]] = (p * inv).astype(BF)
                ds_ref[k, cols[j - 1]] = (p * scaled * (dd[j - 1][ki] - inner)).astype(BF)
        if j > 0:
            out = dot(values_t[...], low_ref[:, cols[j - 1]], 1, 0).astype(BF)
            for t in range(per):
                out_ref[(j - 1) * per + t] = out[:, t * nq:(t + 1) * nq]
            outs.append(out)
    y, z = at_ref[0], at_ref[1]
    for t in range(tile):
        at = t * nq % sub
        wt = dot(outs[t * nq // sub][:, at:at + nq], og_ref[t], 1, 0)
        wt = wt.reshape(NY, NZ, latent // (NY * NZ), wt.shape[1])
        for part_y in range(NY):
            for part_z in range(NZ):
                pieces[part_y ^ y, lax.rem(part_z - z + NZ, NZ), t] = wt[part_y, part_z]

    @pl.when(step < half)
    def _():
        own_a_ref[...] = pieces[0]
        next_a_ref[...] = pieces[3]
        send_a_ref[0] = pieces[1].astype(BF)
        send_a_ref[1] = pieces[2].astype(BF)

    @pl.when(step >= half)
    def _():
        own_b_ref[...] = pieces[0]
        next_b_ref[...] = pieces[1]
        send_b_ref[0] = pieces[3].astype(BF)
        send_b_ref[1] = pieces[2].astype(BF)


def forward(at, parts, bias, qt, dlt, og):
    heads, nq, vd = og.shape
    latent = dlt.shape[1]
    part, feature = parts[0].shape
    wide = (feature + UNIQ + 127) // 128 * 128
    rows = len(parts) * part
    tile = TILE
    steps = heads // tile
    per = steps // 2
    sub = latent // (NY * NZ)
    whole = lambda *shape: pl.BlockSpec(shape, lambda i: (0,) * len(shape))
    cols = lambda n: pl.BlockSpec((n, tile * nq), lambda i: (0, i))
    heads_of = lambda *shape: pl.BlockSpec((tile,) + shape, lambda i: (i, 0, 0))
    at_a = lambda i: jnp.minimum(i, per - 1)
    at_b = lambda i: jnp.maximum(i - per, 0)

    def pieces_at(at):
        one = pl.BlockSpec((NZ, tile, sub, vd), lambda i: (0, at(i), 0, 0))
        two = pl.BlockSpec((2, NZ, tile, sub, vd), lambda i: (0, 0, at(i), 0, 0))
        return [one, one, two]

    shape = jax.ShapeDtypeStruct
    piece_shapes = [
        shape((NZ, heads // 2, sub, vd), F32), shape((NZ, heads // 2, sub, vd), F32),
        shape((2, NZ, heads // 2, sub, vd), BF),
    ]
    return pl.pallas_call(
        forward_kernel,
        grid=(steps,),
        in_specs=[pl.BlockSpec(memory_space=pltpu.SMEM)]
        + [whole(part, feature)] * len(parts)
        + [whole(UNIQ, nq), heads_of(feature, nq), heads_of(latent, nq),
           heads_of(nq, vd)],
        out_specs=[cols(rows), cols(rows), heads_of(latent, nq), whole(rows, wide)]
        + pieces_at(at_a) + pieces_at(at_b),
        out_shape=[
            shape((rows, heads * nq), BF), shape((rows, heads * nq), BF),
            shape((heads, latent, nq), BF), shape((rows, wide), BF),
        ] + piece_shapes * 2,
        scratch_shapes=[pltpu.VMEM((latent, rows), BF), pltpu.VMEM((NY, NZ, tile, sub, vd), F32)],
        compiler_params=pltpu.CompilerParams(vmem_limit_bytes=FORWARD_VMEM),
        cost_estimate=pl.CostEstimate(
            flops=2 * heads * nq * rows * (wide + 2 * latent), bytes_accessed=16_000_000,
            transcendentals=heads * nq * rows,
        ),
    )(at, *parts, bias, qt, dlt, og)


def pool_kernel(low_ref, ds_ref, qt_ref, dlt_ref, near_ref, *far_refs):
    tile, latent, nq = dlt_ref.shape
    feature = near_ref.shape[1]
    rows = near_ref.shape[0]
    refs = (near_ref,) + far_refs

    @pl.when(pl.program_id(0) == 0)
    def _():
        for ref in refs:
            ref[...] = jnp.zeros_like(ref)

    q = jnp.concatenate([qt_ref[t] for t in range(tile)], axis=1)
    dl = jnp.concatenate([dlt_ref[t] for t in range(tile)], axis=1)
    for at in (0, rows):
        ds = ds_ref[at:at + rows]
        low = low_ref[at:at + rows]
        main = dot(ds, q[:latent], 1, 1) + dot(low, dl, 1, 1)
        side = dot(ds, q[latent:], 1, 1)
        refs_here = refs[:1] if at == 0 else refs[1:]
        size = rows // len(refs_here)
        for k, ref in enumerate(refs_here):
            ref[:, :latent] += main[k * size:(k + 1) * size]
            ref[:, latent:] += side[k * size:(k + 1) * size]


def pool_grads(low, ds, qt, dlt):
    rows = low.shape[0]
    heads, feature, nq = qt.shape
    latent = dlt.shape[1]
    tile = TILE
    cols = pl.BlockSpec((rows, tile * nq), lambda i: (0, i))
    heads_of = lambda *shape: pl.BlockSpec((tile,) + shape, lambda i: (i, 0, 0))
    sizes = [rows // 2] + [rows // (2 * NX)] * NX
    return pl.pallas_call(
        pool_kernel,
        grid=(heads // tile,),
        in_specs=[cols, cols, heads_of(feature, nq), heads_of(latent, nq)],
        out_specs=[pl.BlockSpec((n, feature), lambda i: (0, 0)) for n in sizes],
        out_shape=[jax.ShapeDtypeStruct((n, feature), F32) for n in sizes],
        compiler_params=pltpu.CompilerParams(vmem_limit_bytes=POOL_VMEM),
        cost_estimate=pl.CostEstimate(
            flops=2 * heads * nq * rows * (feature + latent), bytes_accessed=12_000_000,
            transcendentals=0,
        ),
    )(low, ds, qt, dlt)


def rest_kernel(ds_ref, keys_ref, out_ref, w_ref, dq_ref, ho_ref):
    tile, feature, nq = dq_ref.shape
    dq = dot(keys_ref[...], ds_ref[...], 0, 0)[:feature].astype(BF)
    for t in range(tile):
        dq_ref[t] = dq[:, t * nq:(t + 1) * nq]
        ho_ref[t] = dot(out_ref[t], w_ref[t], 0, 0).astype(BF)


def rest(ds, keys, out, w, feature):
    heads, latent, vd = w.shape
    rows, wide = keys.shape
    nq = out.shape[2]
    tile = TILE
    heads_of = lambda *shape: pl.BlockSpec((tile,) + shape, lambda i: (i, 0, 0))
    return pl.pallas_call(
        rest_kernel,
        grid=(heads // tile,),
        in_specs=[pl.BlockSpec((rows, tile * nq), lambda i: (0, i)),
                  pl.BlockSpec((rows, wide), lambda i: (0, 0)), heads_of(latent, nq),
                  heads_of(latent, vd)],
        out_specs=[heads_of(feature, nq), heads_of(nq, vd)],
        out_shape=[jax.ShapeDtypeStruct((heads, feature, nq), BF),
                   jax.ShapeDtypeStruct((heads, nq, vd), BF)],
        compiler_params=pltpu.CompilerParams(vmem_limit_bytes=REST_VMEM),
        cost_estimate=pl.CostEstimate(
            flops=1_000_000, bytes_accessed=100_000, transcendentals=0
        ),
    )(ds, keys, out, w)


def settle_kernel(asked_ref, returned_ref, out_ref, total):
    total[...] = jnp.zeros_like(total)

    def add(at, carry):
        slot = asked_ref[at]

        @pl.when(slot >= 0)
        def _():
            total[slot] += returned_ref[at].astype(F32)

        return carry

    lax.fori_loop(0, returned_ref.shape[0], add, 0)
    out_ref[...] = total[...].astype(BF)


def settle(asked, returned, blk_dev):
    _, share, feature = returned.shape
    return pl.pallas_call(
        settle_kernel,
        in_specs=[pl.BlockSpec(memory_space=pltpu.SMEM), pl.BlockSpec(memory_space=pltpu.VMEM)],
        out_specs=pl.BlockSpec(memory_space=pltpu.VMEM),
        out_shape=jax.ShapeDtypeStruct((blk_dev, share, feature), BF),
        scratch_shapes=[pltpu.VMEM((blk_dev, share, feature), F32)],
        cost_estimate=pl.CostEstimate(flops=500_000, bytes_accessed=1_000_000, transcendentals=0),
    )(asked, returned)


def by_ctx(move):
    return [(y * NZ + z, move(y) * NZ + z) for y in range(NY) for z in range(NZ)]


def to_z(k):
    return [(y * NZ + z, y * NZ + (z + k) % NZ) for y in range(NY) for z in range(NZ)]


def by_head(move):
    return [(x * NC + c, move(x, c)) for x in range(NX) for c in range(NC)]


def to_x(k):
    return by_head(lambda x, c: (x + k) % NX * NC + c)


def from_x(k):
    return by_head(lambda x, c: (x - k) % NX * NC + c)


OTHER_CORE = by_head(lambda x, c: x * NC + 1 - c)


def body(latent_cache, queries, selected, block_home, w_uv, out_grad):
    owners = NY * NZ
    blk_dev, block_len, feature = latent_cache.shape
    latent = w_uv.shape[1]
    total = block_home.shape[0]
    nq, heads, _ = queries.shape
    share = block_len // (NX * NC)
    head_at = lax.axis_index("head")
    ctx_at = lax.axis_index("ctx").astype(jnp.int32)

    flat = selected.reshape(-1)
    flat_home = jnp.sum(
        jnp.where(flat[:, None] == jnp.arange(total)[None, :], block_home[None, :], 0), axis=1
    )
    slots = jnp.arange(blk_dev, dtype=jnp.int32)[None, :]
    stored = jnp.arange(total, dtype=jnp.int32).reshape(owners, blk_dev)
    present = jnp.max(
        (flat_home[:, None, None] == stored[None]).astype(jnp.int32), axis=0
    )
    first = jnp.min(jnp.where(present > 0, slots, blk_dev), axis=1)
    last = jnp.max(jnp.where(present > 0, slots, -1), axis=1)
    request = jnp.stack(
        [jnp.where(first < blk_dev, first, -1), jnp.where(last > first, last, -1)], axis=1
    )
    asked = lax.all_to_all(request, "ctx", split_axis=0, concat_axis=0, tiled=True)

    q_t = jnp.transpose(queries, (1, 2, 0))
    og_heads = jnp.swapaxes(out_grad, 0, 1)
    mine = lax.dynamic_slice_in_dim(latent_cache, head_at * share, share, axis=1)
    asked, og_heads, mine = lax.optimization_barrier((asked, og_heads, mine))
    asked = asked.reshape(-1)

    outgoing = mine[jnp.maximum(asked, 0)]
    arrived = lax.all_to_all(
        outgoing.reshape(owners, CAP, share, feature), "ctx", split_axis=0, concat_axis=0, tiled=True
    ).reshape(owners * CAP, share, feature)

    valid = (request >= 0).reshape(-1)
    count = jnp.arange(owners * CAP)
    place = jnp.sum((valid[None, :] & (count[None, :] < count[:, None])).astype(jnp.int32), axis=1)
    hit = valid[None, :] & (place[None, :] == jnp.arange(UNIQ)[:, None])
    source = jnp.sum(jnp.where(hit, count[None, :], 0), axis=1)
    slot_home = (jnp.arange(owners)[:, None] * blk_dev + jnp.maximum(request, 0)).reshape(-1)
    pool_home = jnp.sum(jnp.where(hit, slot_home[None, :], 0), axis=1)
    chosen = jnp.max(
        (flat_home.reshape(nq, -1)[:, :, None] == pool_home[None, None, :]).astype(jnp.int32), axis=1
    )
    spot = jnp.minimum(place, UNIQ - 1)

    bias = jnp.where(chosen > 0, 0.0, OUTSIDE).astype(BF).T
    d_latent = jnp.einsum(
        "hcv,hqv->hcq", w_uv, og_heads, preferred_element_type=F32
    ).astype(BF)
    arrived, bias, d_latent, source, spot = lax.optimization_barrier(
        (arrived, bias, d_latent, source, spot)
    )

    own = arrived[source].reshape(UNIQ * share, feature)
    parts = [own] + [lax.ppermute(own, "head", from_x(k)) for k in range(1, NX)]
    parts = parts + [lax.ppermute(part, "head", OTHER_CORE) for part in parts]

    low, ds, out, keys, own_a, next_a, send_a, own_b, next_b, send_b = forward(
        jnp.stack([ctx_at // NZ, ctx_at % NZ]), parts, bias, q_t, d_latent, og_heads
    )

    flip, turn = by_ctx(lambda y: y ^ 1), by_ctx(lambda y: y ^ 3)
    got_a = lax.ppermute(send_a, "ctx", flip)
    got_b = lax.ppermute(send_b, "ctx", turn)

    near, *far = pool_grads(low, ds, q_t, d_latent)
    far_in = [lax.ppermute(part, "head", OTHER_CORE) for part in far]
    size = UNIQ * share
    quarter = [near[k * size:(k + 1) * size] + far_in[k] for k in range(NX)]
    ahead = {k: lax.ppermute(quarter[k].astype(BF), "head", to_x(k)) for k in (2, 1, 3)}
    summed = quarter[0]
    for k in range(1, NX):
        summed = summed + ahead[k].astype(F32)
    outbound = summed.astype(BF).reshape(UNIQ, share, feature)[spot]
    returned = lax.all_to_all(
        outbound.reshape(owners, CAP, share, feature), "ctx", split_axis=0, concat_axis=0, tiled=True
    ).reshape(owners * CAP, share, feature)

    got_a, got_b, _ = lax.optimization_barrier((got_a, got_b, outbound))
    pass_a = (next_a + got_a[1].astype(F32)).astype(BF)
    pass_b = (next_b + got_b[1].astype(F32)).astype(BF)
    last_a = lax.ppermute(pass_a, "ctx", turn)
    last_b = lax.ppermute(pass_b, "ctx", flip)
    column = jnp.concatenate(
        [
            own_a + got_a[0].astype(F32) + last_a.astype(F32),
            own_b + got_b[0].astype(F32) + last_b.astype(F32),
        ],
        axis=1,
    )
    weight_sum = column[0]
    for k in (4, 3, 5, 2, 6, 1, 7):
        weight_sum = weight_sum + lax.ppermute(column[k].astype(BF), "ctx", to_z(k)).astype(F32)
    weight_grad = weight_sum.astype(BF)

    ds, out, _ = lax.optimization_barrier((ds, out, outbound))
    d_query, out_heads = rest(ds, keys, out, w_uv, feature)
    d_query, out_heads = jnp.transpose(d_query, (2, 0, 1)), jnp.swapaxes(out_heads, 0, 1)
    cache_grad = settle(asked, returned, blk_dev)
    return out_heads, d_query, cache_grad, weight_grad


def solution(mesh):
    in_specs = (
        P("ctx", None, None),
        P("ctx", "head", None),
        P("ctx", None),
        P(),
        P("head", None, None),
        P("ctx", "head", None),
    )
    out_specs = (
        P("ctx", "head", None),
        P("ctx", "head", None),
        P("ctx", "head", None),
        P("head", "ctx", None),
    )
    return jax.shard_map(body, mesh=mesh, in_specs=in_specs, out_specs=out_specs, check_vma=False)
```

```python
import jax
import jax.numpy as jnp
from jax import lax
from jax.experimental import pallas as pl
from jax.experimental.pallas import tpu as pltpu
from jax.sharding import PartitionSpec as P

NY, NZ, NX, NC = 4, 8, 4, 2
UNIQ = 16
CAP = 2
OUTSIDE = -1.0e6
TILE = 4
SUB = 2
CHUNK = 256
POOL_COLS = 512
FORWARD_VMEM = 56 * 1024 * 1024
REST_VMEM = 56 * 1024 * 1024

softmax_scale = 192.0 ** (-0.5)
LOG2E = 1.4426950408889634

BF = jnp.bfloat16
F32 = jnp.float32


def dot(a, b, ca, cb):
    return lax.dot_general(a, b, (((ca,), (cb,)), ((), ())), preferred_element_type=F32)


def forward_kernel(
    at_ref, k0_ref, k1_ref, k2_ref, k3_ref, k4_ref, k5_ref, k6_ref, k7_ref, bias_ref, qt_ref,
    dlt_ref, og_ref, ds_ref, out_ref, keys_ref, own_a_ref, next_a_ref, send_a_ref,
    own_b_ref, next_b_ref, send_b_ref, near_ref, f0_ref, f1_ref, f2_ref, f3_ref,
    values_t, pieces, low_ref,
):
    step = pl.program_id(0)
    tile, nq, _ = og_ref.shape
    wide = keys_ref.shape[1]
    rows, feature = keys_ref.shape[0], k0_ref.shape[1]
    latent = dlt_ref.shape[1]
    part = k0_ref.shape[0]
    group = part // UNIQ
    half = pl.num_programs(0) // 2
    pool_refs = (near_ref, f0_ref, f1_ref, f2_ref, f3_ref)

    @pl.when(step == 0)
    def _():
        for at, ref in enumerate((k0_ref, k1_ref, k2_ref, k3_ref, k4_ref, k5_ref, k6_ref, k7_ref)):
            keys_ref[at * part:(at + 1) * part, :feature] = ref[...]
        owner = (lax.broadcasted_iota(jnp.int32, (rows, wide - feature), 0) // group) % UNIQ
        lane = lax.broadcasted_iota(jnp.int32, (rows, wide - feature), 1)
        keys_ref[:, feature:] = (owner == lane).astype(F32).astype(BF)
        values_t[...] = keys_ref[:, :latent].T
        for ref in pool_refs:
            ref[...] = jnp.zeros_like(ref)

    per = min(SUB, tile)
    sub = per * nq
    rest = jnp.zeros((wide - feature - UNIQ, sub), BF)
    bias = jnp.concatenate([bias_ref[...]] * per, axis=1)

    def scored(j):
        q = jnp.concatenate([qt_ref[j * per + t] for t in range(per)], axis=1)
        return jnp.concatenate([q, bias, rest], axis=0)

    def carried(j):
        return jnp.concatenate([dlt_ref[j * per + t] for t in range(per)], axis=1)

    cols = [slice(at, at + sub) for at in range(0, tile * nq, sub)]
    rate = softmax_scale * LOG2E
    outs, qs, dls = [], [], []
    chunks = [slice(k, k + CHUNK) for k in range(0, rows, CHUNK)]
    def top_of(s):
        t = s[0].max(axis=0, keepdims=True)
        for x in s[1:]:
            t = jnp.maximum(t, x.max(axis=0, keepdims=True))
        return t * rate
    n = len(cols)
    ss, dd, pp = [None] * n, [None] * n, [None] * n
    for j in range(n + 1):
        if j < n:
            ss[j], dd[j] = [], []
            q, dl = scored(j), carried(j)
            qs.append(q)
            dls.append(dl)
        if j > 0:
            pp[j - 1], total, inner = [], 0.0, 0.0
            top = top_of(ss[j - 1])
        for ki, k in enumerate(chunks):
            if j < n:
                ss[j].append(dot(keys_ref[k], q, 1, 0))
            if j > 0:
                p = jnp.exp2(ss[j - 1][ki] * rate - top)
                pp[j - 1].append(p)
                total = total + p.sum(axis=0, keepdims=True)
                inner = inner + (p * dd[j - 1][ki]).sum(axis=0, keepdims=True)
        if j > 0:
            inv = 1.0 / total
            inner = inner * inv
            scaled = inv * softmax_scale
        for ki, k in enumerate(chunks):
            if j < n:
                dd[j].append(dot(keys_ref[k, :latent], dl, 1, 0))
            if j > 0:
                p = pp[j - 1][ki]
                low_ref[k, cols[j - 1]] = (p * inv).astype(BF)
                ds_ref[k, cols[j - 1]] = (p * scaled * (dd[j - 1][ki] - inner)).astype(BF)
        if j > 0:
            out = dot(values_t[...], low_ref[:, cols[j - 1]], 1, 0).astype(BF)
            for t in range(per):
                out_ref[(j - 1) * per + t] = out[:, t * nq:(t + 1) * nq]
            outs.append(out)
    depth = min(POOL_COLS, tile * nq)
    for lo in range(0, tile * nq, depth):
        span = slice(lo, lo + depth)
        here = range(lo // sub, (lo + depth) // sub)
        q = jnp.concatenate([qs[j] for j in here], axis=1)
        dl = jnp.concatenate([dls[j] for j in here], axis=1)
        for k in chunks:
            main = dot(ds_ref[k, span], q[:latent], 1, 1) + dot(low_ref[k, span], dl, 1, 1)
            side = dot(ds_ref[k, span], q[latent:feature], 1, 1)
            at = k.start
            for ref in pool_refs:
                n = ref.shape[0]
                if 0 <= at < n:
                    m = min(n - at, k.stop - k.start)
                    ref[at:at + m, :latent] += main[:m]
                    ref[at:at + m, latent:] += side[:m]
                    main, side, at = main[m:], side[m:], at + m
                    if main.shape[0] == 0:
                        break
                at -= n
    y, z = at_ref[0], at_ref[1]
    for t in range(tile):
        at = t * nq % sub
        wt = dot(outs[t * nq // sub][:, at:at + nq], og_ref[t], 1, 0)
        wt = wt.reshape(NY, NZ, latent // (NY * NZ), wt.shape[1])
        for part_y in range(NY):
            for part_z in range(NZ):
                pieces[part_y ^ y, lax.rem(part_z - z + NZ, NZ), t] = wt[part_y, part_z]

    @pl.when(step < half)
    def _():
        own_a_ref[...] = pieces[0]
        next_a_ref[...] = pieces[3]
        send_a_ref[0] = pieces[1].astype(BF)
        send_a_ref[1] = pieces[2].astype(BF)

    @pl.when(step >= half)
    def _():
        own_b_ref[...] = pieces[0]
        next_b_ref[...] = pieces[1]
        send_b_ref[0] = pieces[3].astype(BF)
        send_b_ref[1] = pieces[2].astype(BF)


def forward(at, parts, bias, qt, dlt, og):
    heads, nq, vd = og.shape
    latent = dlt.shape[1]
    part, feature = parts[0].shape
    wide = (feature + UNIQ + 127) // 128 * 128
    rows = len(parts) * part
    tile = TILE
    steps = heads // tile
    per = steps // 2
    sub = latent // (NY * NZ)
    whole = lambda *shape: pl.BlockSpec(shape, lambda i: (0,) * len(shape))
    cols = lambda n: pl.BlockSpec((n, tile * nq), lambda i: (0, i))
    heads_of = lambda *shape: pl.BlockSpec((tile,) + shape, lambda i: (i, 0, 0))
    at_a = lambda i: jnp.minimum(i, per - 1)
    at_b = lambda i: jnp.maximum(i - per, 0)

    def pieces_at(at):
        one = pl.BlockSpec((NZ, tile, sub, vd), lambda i: (0, at(i), 0, 0))
        two = pl.BlockSpec((2, NZ, tile, sub, vd), lambda i: (0, 0, at(i), 0, 0))
        return [one, one, two]

    sizes = [rows // 2] + [part] * NX
    shape = jax.ShapeDtypeStruct
    piece_shapes = [
        shape((NZ, heads // 2, sub, vd), F32), shape((NZ, heads // 2, sub, vd), F32),
        shape((2, NZ, heads // 2, sub, vd), BF),
    ]
    return pl.pallas_call(
        forward_kernel,
        grid=(steps,),
        in_specs=[pl.BlockSpec(memory_space=pltpu.SMEM)]
        + [whole(part, feature)] * len(parts)
        + [whole(UNIQ, nq), heads_of(feature, nq), heads_of(latent, nq),
           heads_of(nq, vd)],
        out_specs=[cols(rows), heads_of(latent, nq), whole(rows, wide)]
        + pieces_at(at_a) + pieces_at(at_b) + [whole(n, feature) for n in sizes],
        out_shape=[
            shape((rows, heads * nq), BF),
            shape((heads, latent, nq), BF), shape((rows, wide), BF),
        ] + piece_shapes * 2 + [shape((n, feature), F32) for n in sizes],
        scratch_shapes=[
            pltpu.VMEM((latent, rows), BF), pltpu.VMEM((NY, NZ, tile, sub, vd), F32),
            pltpu.VMEM((rows, tile * nq), BF),
        ],
        compiler_params=pltpu.CompilerParams(vmem_limit_bytes=FORWARD_VMEM),
        cost_estimate=pl.CostEstimate(
            flops=4 * heads * nq * rows * (wide + 2 * latent), bytes_accessed=16_000_000,
            transcendentals=heads * nq * rows,
        ),
    )(at, *parts, bias, qt, dlt, og)


def rest_kernel(ds_ref, keys_ref, out_ref, w_ref, dq_ref, ho_ref):
    tile, feature, nq = dq_ref.shape
    dq = dot(keys_ref[...], ds_ref[...], 0, 0)[:feature].astype(BF)
    for t in range(tile):
        dq_ref[t] = dq[:, t * nq:(t + 1) * nq]
        ho_ref[t] = dot(out_ref[t], w_ref[t], 0, 0).astype(BF)


def rest(ds, keys, out, w, feature):
    heads, latent, vd = w.shape
    rows, wide = keys.shape
    nq = out.shape[2]
    tile = TILE
    heads_of = lambda *shape: pl.BlockSpec((tile,) + shape, lambda i: (i, 0, 0))
    return pl.pallas_call(
        rest_kernel,
        grid=(heads // tile,),
        in_specs=[pl.BlockSpec((rows, tile * nq), lambda i: (0, i)),
                  pl.BlockSpec((rows, wide), lambda i: (0, 0)), heads_of(latent, nq),
                  heads_of(latent, vd)],
        out_specs=[heads_of(feature, nq), heads_of(nq, vd)],
        out_shape=[jax.ShapeDtypeStruct((heads, feature, nq), BF),
                   jax.ShapeDtypeStruct((heads, nq, vd), BF)],
        compiler_params=pltpu.CompilerParams(vmem_limit_bytes=REST_VMEM),
        cost_estimate=pl.CostEstimate(
            flops=1_000_000, bytes_accessed=100_000, transcendentals=0
        ),
    )(ds, keys, out, w)


def settle_kernel(asked_ref, returned_ref, out_ref, total):
    total[...] = jnp.zeros_like(total)

    def add(at, carry):
        slot = asked_ref[at]

        @pl.when(slot >= 0)
        def _():
            total[slot] += returned_ref[at].astype(F32)

        return carry

    lax.fori_loop(0, returned_ref.shape[0], add, 0)
    out_ref[...] = total[...].astype(BF)


def settle(asked, returned, blk_dev):
    _, share, feature = returned.shape
    return pl.pallas_call(
        settle_kernel,
        in_specs=[pl.BlockSpec(memory_space=pltpu.SMEM), pl.BlockSpec(memory_space=pltpu.VMEM)],
        out_specs=pl.BlockSpec(memory_space=pltpu.VMEM),
        out_shape=jax.ShapeDtypeStruct((blk_dev, share, feature), BF),
        scratch_shapes=[pltpu.VMEM((blk_dev, share, feature), F32)],
        cost_estimate=pl.CostEstimate(flops=500_000, bytes_accessed=1_000_000, transcendentals=0),
    )(asked, returned)


def by_ctx(move):
    return [(y * NZ + z, move(y) * NZ + z) for y in range(NY) for z in range(NZ)]


def to_z(k):
    return [(y * NZ + z, y * NZ + (z + k) % NZ) for y in range(NY) for z in range(NZ)]


def by_head(move):
    return [(x * NC + c, move(x, c)) for x in range(NX) for c in range(NC)]


def to_x(k):
    return by_head(lambda x, c: (x + k) % NX * NC + c)


def from_x(k):
    return by_head(lambda x, c: (x - k) % NX * NC + c)


OTHER_CORE = by_head(lambda x, c: x * NC + 1 - c)


def body(latent_cache, queries, selected, block_home, w_uv, out_grad):
    owners = NY * NZ
    blk_dev, block_len, feature = latent_cache.shape
    latent = w_uv.shape[1]
    total = block_home.shape[0]
    nq, heads, _ = queries.shape
    share = block_len // (NX * NC)
    head_at = lax.axis_index("head")
    ctx_at = lax.axis_index("ctx").astype(jnp.int32)

    flat = selected.reshape(-1)
    flat_home = jnp.sum(
        jnp.where(flat[:, None] == jnp.arange(total)[None, :], block_home[None, :], 0), axis=1
    )
    slots = jnp.arange(blk_dev, dtype=jnp.int32)[None, :]
    stored = jnp.arange(total, dtype=jnp.int32).reshape(owners, blk_dev)
    present = jnp.max(
        (flat_home[:, None, None] == stored[None]).astype(jnp.int32), axis=0
    )
    first = jnp.min(jnp.where(present > 0, slots, blk_dev), axis=1)
    last = jnp.max(jnp.where(present > 0, slots, -1), axis=1)
    request = jnp.stack(
        [jnp.where(first < blk_dev, first, -1), jnp.where(last > first, last, -1)], axis=1
    )
    asked = lax.all_to_all(request, "ctx", split_axis=0, concat_axis=0, tiled=True)

    q_t = jnp.transpose(queries, (1, 2, 0))
    og_heads = jnp.swapaxes(out_grad, 0, 1)
    mine = lax.dynamic_slice_in_dim(latent_cache, head_at * share, share, axis=1)
    asked, og_heads, mine = lax.optimization_barrier((asked, og_heads, mine))
    asked = asked.reshape(-1)

    outgoing = mine[jnp.maximum(asked, 0)]
    arrived = lax.all_to_all(
        outgoing.reshape(owners, CAP, share, feature), "ctx", split_axis=0, concat_axis=0, tiled=True
    ).reshape(owners * CAP, share, feature)

    valid = (request >= 0).reshape(-1)
    count = jnp.arange(owners * CAP)
    place = jnp.sum((valid[None, :] & (count[None, :] < count[:, None])).astype(jnp.int32), axis=1)
    hit = valid[None, :] & (place[None, :] == jnp.arange(UNIQ)[:, None])
    source = jnp.sum(jnp.where(hit, count[None, :], 0), axis=1)
    slot_home = (jnp.arange(owners)[:, None] * blk_dev + jnp.maximum(request, 0)).reshape(-1)
    pool_home = jnp.sum(jnp.where(hit, slot_home[None, :], 0), axis=1)
    chosen = jnp.max(
        (flat_home.reshape(nq, -1)[:, :, None] == pool_home[None, None, :]).astype(jnp.int32), axis=1
    )
    spot = jnp.minimum(place, UNIQ - 1)

    bias = jnp.where(chosen > 0, 0.0, OUTSIDE).astype(BF).T
    d_latent = jnp.einsum(
        "hcv,hqv->hcq", w_uv, og_heads, preferred_element_type=F32
    ).astype(BF)
    arrived, bias, d_latent, source, spot = lax.optimization_barrier(
        (arrived, bias, d_latent, source, spot)
    )

    own = arrived[source].reshape(UNIQ * share, feature)
    parts = [own] + [lax.ppermute(own, "head", from_x(k)) for k in range(1, NX)]
    parts = parts + [lax.ppermute(part, "head", OTHER_CORE) for part in parts]

    ds, out, keys, own_a, next_a, send_a, own_b, next_b, send_b, near, *far = forward(
        jnp.stack([ctx_at // NZ, ctx_at % NZ]), parts, bias, q_t, d_latent, og_heads
    )

    flip, turn = by_ctx(lambda y: y ^ 1), by_ctx(lambda y: y ^ 3)
    got_a = lax.ppermute(send_a, "ctx", flip)
    got_b = lax.ppermute(send_b, "ctx", turn)

    far_in = [lax.ppermute(part, "head", OTHER_CORE) for part in far]
    size = UNIQ * share
    quarter = [near[k * size:(k + 1) * size] + far_in[k] for k in range(NX)]
    leaving = [part.astype(BF) for part in quarter[1:]]
    ahead = [lax.ppermute(part, "head", to_x(k + 1)) for k, part in enumerate(leaving)]

    ds, out, _, own_quarter = lax.optimization_barrier((ds, out, leaving, quarter[0]))
    d_query, out_heads = rest(ds, keys, out, w_uv, feature)
    ahead, d_query, out_heads = lax.optimization_barrier((ahead, d_query, out_heads))
    summed = own_quarter
    for part in ahead:
        summed = summed + part.astype(F32)
    outbound = summed.astype(BF).reshape(UNIQ, share, feature)[spot]
    returned = lax.all_to_all(
        outbound.reshape(owners, CAP, share, feature), "ctx", split_axis=0, concat_axis=0, tiled=True
    ).reshape(owners * CAP, share, feature)

    got_a, got_b, _ = lax.optimization_barrier((got_a, got_b, outbound))
    pass_a = (next_a + got_a[1].astype(F32)).astype(BF)
    pass_b = (next_b + got_b[1].astype(F32)).astype(BF)
    last_a = lax.ppermute(pass_a, "ctx", turn)
    last_b = lax.ppermute(pass_b, "ctx", flip)

    column = jnp.concatenate(
        [
            own_a + got_a[0].astype(F32) + last_a.astype(F32),
            own_b + got_b[0].astype(F32) + last_b.astype(F32),
        ],
        axis=1,
    )
    weight_sum = column[0]
    for k in (4, 3, 5, 2, 6, 1, 7):
        weight_sum = weight_sum + lax.ppermute(column[k].astype(BF), "ctx", to_z(k)).astype(F32)
    weight_grad = weight_sum.astype(BF)

    cache_grad = settle(asked, returned, blk_dev)
    return (
        jnp.swapaxes(out_heads, 0, 1), jnp.transpose(d_query, (2, 0, 1)), cache_grad, weight_grad
    )


def solution(mesh):
    in_specs = (
        P("ctx", None, None),
        P("ctx", "head", None),
        P("ctx", None),
        P(),
        P("head", None, None),
        P("ctx", "head", None),
    )
    out_specs = (
        P("ctx", "head", None),
        P("ctx", "head", None),
        P("ctx", "head", None),
        P("head", "ctx", None),
    )
    return jax.shard_map(body, mesh=mesh, in_specs=in_specs, out_specs=out_specs, check_vma=False)
```

```python
import jax
import jax.numpy as jnp
from jax import lax
from jax.experimental import pallas as pl
from jax.experimental.pallas import tpu as pltpu
from jax.sharding import PartitionSpec as P

NY, NZ, NX, NC = 4, 8, 4, 2
UNIQ = 16
CAP = 2
OUTSIDE = -1.0e6
TILE = 4
SUB = 2
CHUNK = 256
POOL_COLS = 512
FORWARD_VMEM = 56 * 1024 * 1024
REST_VMEM = 56 * 1024 * 1024

softmax_scale = 192.0 ** (-0.5)
LOG2E = 1.4426950408889634

BF = jnp.bfloat16
F32 = jnp.float32


def dot(a, b, ca, cb):
    return lax.dot_general(a, b, (((ca,), (cb,)), ((), ())), preferred_element_type=F32)


def forward_kernel(
    at_ref, k0_ref, k1_ref, k2_ref, k3_ref, k4_ref, k5_ref, k6_ref, k7_ref, bias_ref, qt_ref,
    dlt_ref, og_ref, ds_ref, out_ref, keys_ref, own_a_ref, next_a_ref, send_a_ref,
    own_b_ref, next_b_ref, send_b_ref, near_ref, f0_ref, f1_ref, f2_ref, f3_ref,
    values_t, pieces, low_ref,
):
    step = pl.program_id(0)
    tile, nq, _ = og_ref.shape
    wide = keys_ref.shape[1]
    rows, feature = keys_ref.shape[0], k0_ref.shape[1]
    latent = dlt_ref.shape[1]
    part = k0_ref.shape[0]
    group = part // UNIQ
    half = pl.num_programs(0) // 2
    pool_refs = (near_ref, f0_ref, f1_ref, f2_ref, f3_ref)

    @pl.when(step == 0)
    def _():
        for at, ref in enumerate((k0_ref, k1_ref, k2_ref, k3_ref, k4_ref, k5_ref, k6_ref, k7_ref)):
            keys_ref[at * part:(at + 1) * part, :feature] = ref[...]
        owner = (lax.broadcasted_iota(jnp.int32, (rows, wide - feature), 0) // group) % UNIQ
        lane = lax.broadcasted_iota(jnp.int32, (rows, wide - feature), 1)
        keys_ref[:, feature:] = (owner == lane).astype(F32).astype(BF)
        values_t[...] = keys_ref[:, :latent].T
        for ref in pool_refs:
            ref[...] = jnp.zeros_like(ref)

    per = min(SUB, tile)
    sub = per * nq
    rest = jnp.zeros((wide - feature - UNIQ, sub), BF)
    bias = jnp.concatenate([bias_ref[...]] * per, axis=1)

    def scored(j):
        q = jnp.concatenate([qt_ref[j * per + t] for t in range(per)], axis=1)
        return jnp.concatenate([q, bias, rest], axis=0)

    def carried(j):
        return jnp.concatenate([dlt_ref[j * per + t] for t in range(per)], axis=1)

    cols = [slice(at, at + sub) for at in range(0, tile * nq, sub)]
    rate = softmax_scale * LOG2E
    outs, qs, dls = [], [], []
    chunks = [slice(k, k + CHUNK) for k in range(0, rows, CHUNK)]
    def top_of(s):
        t = s[0].max(axis=0, keepdims=True)
        for x in s[1:]:
            t = jnp.maximum(t, x.max(axis=0, keepdims=True))
        return t * rate
    n = len(cols)
    ss, dd, pp = [None] * n, [None] * n, [None] * n
    for j in range(n + 1):
        if j < n:
            ss[j], dd[j] = [], []
            q, dl = scored(j), carried(j)
            qs.append(q)
            dls.append(dl)
        if j > 0:
            pp[j - 1], total, inner = [], 0.0, 0.0
            top = top_of(ss[j - 1])
        for ki, k in enumerate(chunks):
            if j < n:
                ss[j].append(dot(keys_ref[k], q, 1, 0))
            if j > 0:
                p = jnp.exp2(ss[j - 1][ki] * rate - top)
                pp[j - 1].append(p)
                total = total + p.sum(axis=0, keepdims=True)
                inner = inner + (p * dd[j - 1][ki]).sum(axis=0, keepdims=True)
        if j > 0:
            inv = 1.0 / total
            inner = inner * inv
            scaled = inv * softmax_scale
        for ki, k in enumerate(chunks):
            if j < n:
                dd[j].append(dot(keys_ref[k, :latent], dl, 1, 0))
            if j > 0:
                p = pp[j - 1][ki]
                low_ref[k, cols[j - 1]] = (p * inv).astype(BF)
                ds_ref[k, cols[j - 1]] = (p * scaled * (dd[j - 1][ki] - inner)).astype(BF)
        if j > 0:
            out = dot(values_t[...], low_ref[:, cols[j - 1]], 1, 0).astype(BF)
            for t in range(per):
                out_ref[(j - 1) * per + t] = out[:, t * nq:(t + 1) * nq]
            outs.append(out)
    depth = min(POOL_COLS, tile * nq)
    for lo in range(0, tile * nq, depth):
        span = slice(lo, lo + depth)
        here = range(lo // sub, (lo + depth) // sub)
        q = jnp.concatenate([qs[j] for j in here], axis=1)
        dl = jnp.concatenate([dls[j] for j in here], axis=1)
        for k in chunks:
            main = dot(ds_ref[k, span], q[:latent], 1, 1) + dot(low_ref[k, span], dl, 1, 1)
            side = dot(ds_ref[k, span], q[latent:feature], 1, 1)
            at = k.start
            for ref in pool_refs:
                n = ref.shape[0]
                if 0 <= at < n:
                    m = min(n - at, k.stop - k.start)
                    ref[at:at + m, :latent] += main[:m]
                    ref[at:at + m, latent:] += side[:m]
                    main, side, at = main[m:], side[m:], at + m
                    if main.shape[0] == 0:
                        break
                at -= n
    y, z = at_ref[0], at_ref[1]
    for t in range(tile):
        at = t * nq % sub
        wt = dot(outs[t * nq // sub][:, at:at + nq], og_ref[t], 1, 0)
        wt = wt.reshape(NY, NZ, latent // (NY * NZ), wt.shape[1])
        for part_y in range(NY):
            for part_z in range(NZ):
                pieces[part_y ^ y, lax.rem(part_z - z + NZ, NZ), t] = wt[part_y, part_z]

    @pl.when(step < half)
    def _():
        own_a_ref[...] = pieces[0]
        next_a_ref[...] = pieces[3]
        send_a_ref[0] = pieces[1].astype(BF)
        send_a_ref[1] = pieces[2].astype(BF)

    @pl.when(step >= half)
    def _():
        own_b_ref[...] = pieces[0]
        next_b_ref[...] = pieces[1]
        send_b_ref[0] = pieces[3].astype(BF)
        send_b_ref[1] = pieces[2].astype(BF)


def forward(at, parts, bias, qt, dlt, og):
    heads, nq, vd = og.shape
    latent = dlt.shape[1]
    part, feature = parts[0].shape
    wide = (feature + UNIQ + 127) // 128 * 128
    rows = len(parts) * part
    tile = TILE
    steps = heads // tile
    per = steps // 2
    sub = latent // (NY * NZ)
    whole = lambda *shape: pl.BlockSpec(shape, lambda i: (0,) * len(shape))
    cols = lambda n: pl.BlockSpec((n, tile * nq), lambda i: (0, i))
    heads_of = lambda *shape: pl.BlockSpec((tile,) + shape, lambda i: (i, 0, 0))
    at_a = lambda i: jnp.minimum(i, per - 1)
    at_b = lambda i: jnp.maximum(i - per, 0)

    def pieces_at(at):
        one = pl.BlockSpec((NZ, tile, sub, vd), lambda i: (0, at(i), 0, 0))
        two = pl.BlockSpec((2, NZ, tile, sub, vd), lambda i: (0, 0, at(i), 0, 0))
        return [one, one, two]

    sizes = [rows // 2] + [part] * NX
    shape = jax.ShapeDtypeStruct
    piece_shapes = [
        shape((NZ, heads // 2, sub, vd), F32), shape((NZ, heads // 2, sub, vd), F32),
        shape((2, NZ, heads // 2, sub, vd), BF),
    ]
    return pl.pallas_call(
        forward_kernel,
        grid=(steps,),
        in_specs=[pl.BlockSpec(memory_space=pltpu.SMEM)]
        + [whole(part, feature)] * len(parts)
        + [whole(UNIQ, nq), heads_of(feature, nq), heads_of(latent, nq),
           heads_of(nq, vd)],
        out_specs=[cols(rows), heads_of(latent, nq), whole(rows, wide)]
        + pieces_at(at_a) + pieces_at(at_b) + [whole(n, feature) for n in sizes],
        out_shape=[
            shape((rows, heads * nq), BF),
            shape((heads, latent, nq), BF), shape((rows, wide), BF),
        ] + piece_shapes * 2 + [shape((n, feature), F32) for n in sizes],
        scratch_shapes=[
            pltpu.VMEM((latent, rows), BF), pltpu.VMEM((NY, NZ, tile, sub, vd), F32),
            pltpu.VMEM((rows, tile * nq), BF),
        ],
        compiler_params=pltpu.CompilerParams(vmem_limit_bytes=FORWARD_VMEM),
        cost_estimate=pl.CostEstimate(
            flops=4 * heads * nq * rows * (wide + 2 * latent), bytes_accessed=16_000_000,
            transcendentals=heads * nq * rows,
        ),
    )(at, *parts, bias, qt, dlt, og)


def rest_kernel(ds_ref, keys_ref, out_ref, w_ref, dq_ref, ho_ref):
    tile, feature, nq = dq_ref.shape
    dq = dot(keys_ref[...], ds_ref[...], 0, 0)[:feature].astype(BF)
    for t in range(tile):
        dq_ref[t] = dq[:, t * nq:(t + 1) * nq]
        ho_ref[t] = dot(out_ref[t], w_ref[t], 0, 0).astype(BF)


def rest(ds, keys, out, w, feature):
    heads, latent, vd = w.shape
    rows, wide = keys.shape
    nq = out.shape[2]
    tile = TILE
    heads_of = lambda *shape: pl.BlockSpec((tile,) + shape, lambda i: (i, 0, 0))
    return pl.pallas_call(
        rest_kernel,
        grid=(heads // tile,),
        in_specs=[pl.BlockSpec((rows, tile * nq), lambda i: (0, i)),
                  pl.BlockSpec((rows, wide), lambda i: (0, 0)), heads_of(latent, nq),
                  heads_of(latent, vd)],
        out_specs=[heads_of(feature, nq), heads_of(nq, vd)],
        out_shape=[jax.ShapeDtypeStruct((heads, feature, nq), BF),
                   jax.ShapeDtypeStruct((heads, nq, vd), BF)],
        compiler_params=pltpu.CompilerParams(vmem_limit_bytes=REST_VMEM),
        cost_estimate=pl.CostEstimate(
            flops=1_000_000, bytes_accessed=100_000, transcendentals=0
        ),
    )(ds, keys, out, w)


def settle_kernel(asked_ref, returned_ref, out_ref, total):
    total[...] = jnp.zeros_like(total)

    def add(at, carry):
        slot = asked_ref[at]

        @pl.when(slot >= 0)
        def _():
            total[slot] += returned_ref[at].astype(F32)

        return carry

    lax.fori_loop(0, returned_ref.shape[0], add, 0)
    out_ref[...] = total[...].astype(BF)


def settle(asked, returned, blk_dev):
    _, share, feature = returned.shape
    return pl.pallas_call(
        settle_kernel,
        in_specs=[pl.BlockSpec(memory_space=pltpu.SMEM), pl.BlockSpec(memory_space=pltpu.VMEM)],
        out_specs=pl.BlockSpec(memory_space=pltpu.VMEM),
        out_shape=jax.ShapeDtypeStruct((blk_dev, share, feature), BF),
        scratch_shapes=[pltpu.VMEM((blk_dev, share, feature), F32)],
        cost_estimate=pl.CostEstimate(flops=500_000, bytes_accessed=1_000_000, transcendentals=0),
    )(asked, returned)


def by_ctx(move):
    return [(y * NZ + z, move(y) * NZ + z) for y in range(NY) for z in range(NZ)]


def to_z(k):
    return [(y * NZ + z, y * NZ + (z + k) % NZ) for y in range(NY) for z in range(NZ)]


def by_head(move):
    return [(x * NC + c, move(x, c)) for x in range(NX) for c in range(NC)]


def to_x(k):
    return by_head(lambda x, c: (x + k) % NX * NC + c)


def from_x(k):
    return by_head(lambda x, c: (x - k) % NX * NC + c)


OTHER_CORE = by_head(lambda x, c: x * NC + 1 - c)


def body(latent_cache, queries, selected, block_home, w_uv, out_grad):
    owners = NY * NZ
    blk_dev, block_len, feature = latent_cache.shape
    latent = w_uv.shape[1]
    total = block_home.shape[0]
    nq, heads, _ = queries.shape
    share = block_len // (NX * NC)
    head_at = lax.axis_index("head")
    ctx_at = lax.axis_index("ctx").astype(jnp.int32)

    flat = selected.reshape(-1)
    flat_home = jnp.sum(
        jnp.where(flat[:, None] == jnp.arange(total)[None, :], block_home[None, :], 0), axis=1
    )
    slots = jnp.arange(blk_dev, dtype=jnp.int32)[None, :]
    stored = jnp.arange(total, dtype=jnp.int32).reshape(owners, blk_dev)
    present = jnp.max(
        (flat_home[:, None, None] == stored[None]).astype(jnp.int32), axis=0
    )
    first = jnp.min(jnp.where(present > 0, slots, blk_dev), axis=1)
    last = jnp.max(jnp.where(present > 0, slots, -1), axis=1)
    request = jnp.stack(
        [jnp.where(first < blk_dev, first, -1), jnp.where(last > first, last, -1)], axis=1
    )
    asked = lax.all_to_all(request, "ctx", split_axis=0, concat_axis=0, tiled=True)

    q_t = jnp.transpose(queries, (1, 2, 0))
    og_heads = jnp.swapaxes(out_grad, 0, 1)
    mine = lax.dynamic_slice_in_dim(latent_cache, head_at * share, share, axis=1)
    asked, og_heads, mine = lax.optimization_barrier((asked, og_heads, mine))
    asked = asked.reshape(-1)

    outgoing = mine[jnp.maximum(asked, 0)]
    arrived = lax.all_to_all(
        outgoing.reshape(owners, CAP, share, feature), "ctx", split_axis=0, concat_axis=0, tiled=True
    ).reshape(owners * CAP, share, feature)

    valid = (request >= 0).reshape(-1)
    count = jnp.arange(owners * CAP)
    place = jnp.sum((valid[None, :] & (count[None, :] < count[:, None])).astype(jnp.int32), axis=1)
    hit = valid[None, :] & (place[None, :] == jnp.arange(UNIQ)[:, None])
    source = jnp.sum(jnp.where(hit, count[None, :], 0), axis=1)
    slot_home = (jnp.arange(owners)[:, None] * blk_dev + jnp.maximum(request, 0)).reshape(-1)
    pool_home = jnp.sum(jnp.where(hit, slot_home[None, :], 0), axis=1)
    chosen = jnp.max(
        (flat_home.reshape(nq, -1)[:, :, None] == pool_home[None, None, :]).astype(jnp.int32), axis=1
    )
    spot = jnp.minimum(place, UNIQ - 1)

    bias = jnp.where(chosen > 0, 0.0, OUTSIDE).astype(BF).T
    d_latent = jnp.einsum(
        "hcv,hqv->hcq", w_uv, og_heads, preferred_element_type=F32
    ).astype(BF)
    arrived, bias, d_latent, source, spot = lax.optimization_barrier(
        (arrived, bias, d_latent, source, spot)
    )

    own = arrived[source].reshape(UNIQ * share, feature)
    parts = [own] + [lax.ppermute(own, "head", from_x(k)) for k in range(1, NX)]
    parts = parts + [lax.ppermute(part, "head", OTHER_CORE) for part in parts]

    ds, out, keys, own_a, next_a, send_a, own_b, next_b, send_b, near, *far = forward(
        jnp.stack([ctx_at // NZ, ctx_at % NZ]), parts, bias, q_t, d_latent, og_heads
    )

    flip, turn = by_ctx(lambda y: y ^ 1), by_ctx(lambda y: y ^ 3)
    got_a = lax.ppermute(send_a, "ctx", flip)
    got_b = lax.ppermute(send_b, "ctx", turn)

    far_in = [lax.ppermute(part, "head", OTHER_CORE) for part in far]
    size = UNIQ * share
    quarter = [near[k * size:(k + 1) * size] + far_in[k] for k in range(NX)]
    leaving = [part.astype(BF) for part in quarter[1:]]
    ahead = [lax.ppermute(part, "head", to_x(k + 1)) for k, part in enumerate(leaving)]

    ds, out, _, own_quarter = lax.optimization_barrier((ds, out, leaving, quarter[0]))
    d_query, out_heads = rest(ds, keys, out, w_uv, feature)
    ahead, got_a, got_b, d_query, out_heads = lax.optimization_barrier(
        (ahead, got_a, got_b, d_query, out_heads)
    )

    pass_a = (next_a + got_a[1].astype(F32)).astype(BF)
    pass_b = (next_b + got_b[1].astype(F32)).astype(BF)
    pass_a, pass_b = lax.optimization_barrier((pass_a, pass_b))
    last_a = lax.ppermute(pass_a, "ctx", turn)
    last_b = lax.ppermute(pass_b, "ctx", flip)

    ahead, own_quarter, out_heads, _, _ = lax.optimization_barrier(
        (ahead, own_quarter, out_heads, pass_a, pass_b)
    )
    summed = own_quarter
    for part in ahead:
        summed = summed + part.astype(F32)
    outbound = summed.astype(BF).reshape(UNIQ, share, feature)[spot]
    head_out = jnp.swapaxes(out_heads, 0, 1)
    outbound, head_out, last_a, last_b = lax.optimization_barrier(
        (outbound, head_out, last_a, last_b)
    )
    returned = lax.all_to_all(
        outbound.reshape(owners, CAP, share, feature), "ctx", split_axis=0, concat_axis=0, tiled=True
    ).reshape(owners * CAP, share, feature)

    column = jnp.concatenate(
        [
            own_a + got_a[0].astype(F32) + last_a.astype(F32),
            own_b + got_b[0].astype(F32) + last_b.astype(F32),
        ],
        axis=1,
    )
    weight_sum = column[0]
    for k in (4, 3, 5, 2, 6, 1, 7):
        weight_sum = weight_sum + lax.ppermute(column[k].astype(BF), "ctx", to_z(k)).astype(F32)
    weight_grad = weight_sum.astype(BF)

    cache_grad = settle(asked, returned, blk_dev)
    return (
        head_out, jnp.transpose(d_query, (2, 0, 1)), cache_grad, weight_grad
    )


def solution(mesh):
    in_specs = (
        P("ctx", None, None),
        P("ctx", "head", None),
        P("ctx", None),
        P(),
        P("head", None, None),
        P("ctx", "head", None),
    )
    out_specs = (
        P("ctx", "head", None),
        P("ctx", "head", None),
        P("ctx", "head", None),
        P("head", "ctx", None),
    )
    return jax.shard_map(body, mesh=mesh, in_specs=in_specs, out_specs=out_specs, check_vma=False)
```

```python
import jax
import jax.numpy as jnp
from jax import lax
from jax.experimental import pallas as pl
from jax.experimental.pallas import tpu as pltpu
from jax.sharding import PartitionSpec as P

NY, NZ, NX, NC = 4, 8, 4, 2
UNIQ = 16
CAP = 2
OUTSIDE = -1.0e6
TILE = 4
SUB = 2
CHUNK = 256
POOL_COLS = 512
FORWARD_VMEM = 56 * 1024 * 1024
REST_VMEM = 56 * 1024 * 1024

softmax_scale = 192.0 ** (-0.5)
LOG2E = 1.4426950408889634

BF = jnp.bfloat16
F32 = jnp.float32


def dot(a, b, ca, cb):
    return lax.dot_general(a, b, (((ca,), (cb,)), ((), ())), preferred_element_type=F32)


def forward_kernel(
    y_ref, k0_ref, k1_ref, k2_ref, k3_ref, k4_ref, k5_ref, k6_ref, k7_ref, bias_ref, qt_ref,
    dlt_ref, og_ref, ds_ref, out_ref, keys_ref, own_a_ref, next_a_ref, send_a_ref,
    own_b_ref, next_b_ref, send_b_ref, near_ref, f0_ref, f1_ref, f2_ref, f3_ref,
    values_t, pieces, low_ref,
):
    step = pl.program_id(0)
    tile, nq, _ = og_ref.shape
    wide = keys_ref.shape[1]
    rows, feature = keys_ref.shape[0], k0_ref.shape[1]
    latent = dlt_ref.shape[1]
    part = k0_ref.shape[0]
    group = part // UNIQ
    half = pl.num_programs(0) // 2
    pool_refs = (near_ref, f0_ref, f1_ref, f2_ref, f3_ref)

    @pl.when(step == 0)
    def _():
        for at, ref in enumerate((k0_ref, k1_ref, k2_ref, k3_ref, k4_ref, k5_ref, k6_ref, k7_ref)):
            keys_ref[at * part:(at + 1) * part, :feature] = ref[...]
        owner = (lax.broadcasted_iota(jnp.int32, (rows, wide - feature), 0) // group) % UNIQ
        lane = lax.broadcasted_iota(jnp.int32, (rows, wide - feature), 1)
        keys_ref[:, feature:] = (owner == lane).astype(F32).astype(BF)
        values_t[...] = keys_ref[:, :latent].T
        for ref in pool_refs:
            ref[...] = jnp.zeros_like(ref)

    per = min(SUB, tile)
    sub = per * nq
    rest = jnp.zeros((wide - feature - UNIQ, sub), BF)
    bias = jnp.concatenate([bias_ref[...]] * per, axis=1)

    def scored(j):
        q = jnp.concatenate([qt_ref[j * per + t] for t in range(per)], axis=1)
        return jnp.concatenate([q, bias, rest], axis=0)

    def carried(j):
        return jnp.concatenate([dlt_ref[j * per + t] for t in range(per)], axis=1)

    cols = [slice(at, at + sub) for at in range(0, tile * nq, sub)]
    rate = softmax_scale * LOG2E
    outs, qs, dls = [], [], []
    chunks = [slice(k, k + CHUNK) for k in range(0, rows, CHUNK)]
    def top_of(s):
        t = s[0].max(axis=0, keepdims=True)
        for x in s[1:]:
            t = jnp.maximum(t, x.max(axis=0, keepdims=True))
        return t * rate
    n = len(cols)
    ss, dd, pp = [None] * n, [None] * n, [None] * n
    for j in range(n + 1):
        if j < n:
            ss[j], dd[j] = [], []
            q, dl = scored(j), carried(j)
            qs.append(q)
            dls.append(dl)
        if j > 0:
            pp[j - 1], total, inner = [], 0.0, 0.0
            top = top_of(ss[j - 1])
        for ki, k in enumerate(chunks):
            if j < n:
                ss[j].append(dot(keys_ref[k], q, 1, 0))
            if j > 0:
                p = jnp.exp2(ss[j - 1][ki] * rate - top)
                pp[j - 1].append(p)
                total = total + p.sum(axis=0, keepdims=True)
                inner = inner + (p * dd[j - 1][ki]).sum(axis=0, keepdims=True)
        if j > 0:
            inv = 1.0 / total
            inner = inner * inv
            scaled = inv * softmax_scale
        for ki, k in enumerate(chunks):
            if j < n:
                dd[j].append(dot(keys_ref[k, :latent], dl, 1, 0))
            if j > 0:
                p = pp[j - 1][ki]
                low_ref[k, cols[j - 1]] = (p * inv).astype(BF)
                ds_ref[k, cols[j - 1]] = (p * scaled * (dd[j - 1][ki] - inner)).astype(BF)
        if j > 0:
            out = dot(values_t[...], low_ref[:, cols[j - 1]], 1, 0).astype(BF)
            for t in range(per):
                out_ref[(j - 1) * per + t] = out[:, t * nq:(t + 1) * nq]
            outs.append(out)
    depth = min(POOL_COLS, tile * nq)
    for lo in range(0, tile * nq, depth):
        span = slice(lo, lo + depth)
        here = range(lo // sub, (lo + depth) // sub)
        q = jnp.concatenate([qs[j] for j in here], axis=1)
        dl = jnp.concatenate([dls[j] for j in here], axis=1)
        for k in chunks:
            main = dot(ds_ref[k, span], q[:latent], 1, 1) + dot(low_ref[k, span], dl, 1, 1)
            side = dot(ds_ref[k, span], q[latent:feature], 1, 1)
            at = k.start
            for ref in pool_refs:
                n = ref.shape[0]
                if 0 <= at < n:
                    m = min(n - at, k.stop - k.start)
                    ref[at:at + m, :latent] += main[:m]
                    ref[at:at + m, latent:] += side[:m]
                    main, side, at = main[m:], side[m:], at + m
                    if main.shape[0] == 0:
                        break
                at -= n
    y = y_ref[0]
    for t in range(tile):
        at = t * nq % sub
        wt = dot(outs[t * nq // sub][:, at:at + nq], og_ref[t], 1, 0)
        wt = wt.reshape(NY, NZ, latent // (NY * NZ), wt.shape[1])
        for part_y in range(NY):
            pieces[part_y ^ y, :, t] = wt[part_y]

    @pl.when(step < half)
    def _():
        own_a_ref[...] = pieces[0]
        next_a_ref[...] = pieces[3]
        send_a_ref[0] = pieces[1].astype(BF)
        send_a_ref[1] = pieces[2].astype(BF)

    @pl.when(step >= half)
    def _():
        own_b_ref[...] = pieces[0]
        next_b_ref[...] = pieces[1]
        send_b_ref[0] = pieces[3].astype(BF)
        send_b_ref[1] = pieces[2].astype(BF)


def forward(y, parts, bias, qt, dlt, og):
    heads, nq, vd = og.shape
    latent = dlt.shape[1]
    part, feature = parts[0].shape
    wide = (feature + UNIQ + 127) // 128 * 128
    rows = len(parts) * part
    tile = TILE
    steps = heads // tile
    per = steps // 2
    sub = latent // (NY * NZ)
    whole = lambda *shape: pl.BlockSpec(shape, lambda i: (0,) * len(shape))
    cols = lambda n: pl.BlockSpec((n, tile * nq), lambda i: (0, i))
    heads_of = lambda *shape: pl.BlockSpec((tile,) + shape, lambda i: (i, 0, 0))
    at_a = lambda i: jnp.minimum(i, per - 1)
    at_b = lambda i: jnp.maximum(i - per, 0)

    def pieces_at(at):
        one = pl.BlockSpec((NZ, tile, sub, vd), lambda i: (0, at(i), 0, 0))
        two = pl.BlockSpec((2, NZ, tile, sub, vd), lambda i: (0, 0, at(i), 0, 0))
        return [one, one, two]

    sizes = [rows // 2] + [part] * NX
    shape = jax.ShapeDtypeStruct
    piece_shapes = [
        shape((NZ, heads // 2, sub, vd), F32), shape((NZ, heads // 2, sub, vd), F32),
        shape((2, NZ, heads // 2, sub, vd), BF),
    ]
    return pl.pallas_call(
        forward_kernel,
        grid=(steps,),
        in_specs=[pl.BlockSpec(memory_space=pltpu.SMEM)]
        + [whole(part, feature)] * len(parts)
        + [whole(UNIQ, nq), heads_of(feature, nq), heads_of(latent, nq),
           heads_of(nq, vd)],
        out_specs=[cols(rows), heads_of(latent, nq), whole(rows, wide)]
        + pieces_at(at_a) + pieces_at(at_b) + [whole(n, feature) for n in sizes],
        out_shape=[
            shape((rows, heads * nq), BF),
            shape((heads, latent, nq), BF), shape((rows, wide), BF),
        ] + piece_shapes * 2 + [shape((n, feature), F32) for n in sizes],
        scratch_shapes=[
            pltpu.VMEM((latent, rows), BF), pltpu.VMEM((NY, NZ, tile, sub, vd), F32),
            pltpu.VMEM((rows, tile * nq), BF),
        ],
        compiler_params=pltpu.CompilerParams(vmem_limit_bytes=FORWARD_VMEM),
        cost_estimate=pl.CostEstimate(
            flops=4 * heads * nq * rows * (wide + 2 * latent), bytes_accessed=16_000_000,
            transcendentals=heads * nq * rows,
        ),
    )(y, *parts, bias, qt, dlt, og)


def rest_kernel(ds_ref, keys_ref, out_ref, w_ref, dq_ref, ho_ref):
    tile, feature, nq = dq_ref.shape
    dq = dot(keys_ref[...], ds_ref[...], 0, 0)[:feature].astype(BF)
    for t in range(tile):
        dq_ref[t] = dq[:, t * nq:(t + 1) * nq]
        ho_ref[t] = dot(out_ref[t], w_ref[t], 0, 0).astype(BF)


def rest(ds, keys, out, w, feature):
    heads, latent, vd = w.shape
    rows, wide = keys.shape
    nq = out.shape[2]
    tile = TILE
    heads_of = lambda *shape: pl.BlockSpec((tile,) + shape, lambda i: (i, 0, 0))
    return pl.pallas_call(
        rest_kernel,
        grid=(heads // tile,),
        in_specs=[pl.BlockSpec((rows, tile * nq), lambda i: (0, i)),
                  pl.BlockSpec((rows, wide), lambda i: (0, 0)), heads_of(latent, nq),
                  heads_of(latent, vd)],
        out_specs=[heads_of(feature, nq), heads_of(nq, vd)],
        out_shape=[jax.ShapeDtypeStruct((heads, feature, nq), BF),
                   jax.ShapeDtypeStruct((heads, nq, vd), BF)],
        compiler_params=pltpu.CompilerParams(vmem_limit_bytes=REST_VMEM),
        cost_estimate=pl.CostEstimate(
            flops=1_000_000, bytes_accessed=100_000, transcendentals=0
        ),
    )(ds, keys, out, w)


def wanted_kernel(selected_ref, home_ref, out_ref):
    owners = out_ref.shape[0]
    blk_dev = home_ref.shape[0] * home_ref.shape[1] // owners
    names = selected_ref[...].T
    lane = lax.broadcasted_iota(jnp.int32, (names.shape[0], home_ref.shape[1]), 1)
    owner = lax.broadcasted_iota(jnp.int32, (owners, home_ref.shape[1]), 0)
    first = jnp.full(owner.shape, blk_dev, jnp.int32)
    last = jnp.full(owner.shape, -1, jnp.int32)
    for row in range(home_ref.shape[0]):
        named = jnp.zeros(lane.shape, jnp.int32)
        for k in range(names.shape[1]):
            named = jnp.where(names[:, k:k + 1] == lane + row * lane.shape[1], 1, named)
        named = jnp.max(named, axis=0, keepdims=True)
        home = home_ref[row:row + 1, :]
        here = (named > 0) & (lax.div(home, blk_dev) == owner)
        slot = lax.rem(home, blk_dev)
        first = jnp.minimum(first, jnp.where(here, slot, blk_dev))
        last = jnp.maximum(last, jnp.where(here, slot, -1))
    first = jnp.min(first, axis=1, keepdims=True)
    last = jnp.max(last, axis=1, keepdims=True)
    column = lax.broadcasted_iota(jnp.int32, out_ref.shape, 1)
    second = jnp.where(last > first, last, -1)
    out_ref[...] = jnp.where(column == 0, jnp.where(first < blk_dev, first, -1), second)


def wanted(selected_t, block_home, owners, blk_dev):
    vm = pl.BlockSpec(memory_space=pltpu.VMEM)
    return pl.pallas_call(
        wanted_kernel,
        in_specs=[vm, vm],
        out_specs=vm,
        out_shape=jax.ShapeDtypeStruct((owners, CAP), jnp.int32),
        cost_estimate=pl.CostEstimate(flops=3_000_000, bytes_accessed=10_000, transcendentals=0),
    )(selected_t, block_home.reshape(-1, 128))


def settle_kernel(asked_ref, returned_ref, out_ref, total):
    total[...] = jnp.zeros_like(total)

    def add(at, carry):
        slot = asked_ref[at]

        @pl.when(slot >= 0)
        def _():
            total[slot] += returned_ref[at].astype(F32)

        return carry

    lax.fori_loop(0, returned_ref.shape[0], add, 0)
    out_ref[...] = total[...].astype(BF)


def settle(asked, returned, blk_dev):
    _, share, feature = returned.shape
    return pl.pallas_call(
        settle_kernel,
        in_specs=[pl.BlockSpec(memory_space=pltpu.SMEM), pl.BlockSpec(memory_space=pltpu.VMEM)],
        out_specs=pl.BlockSpec(memory_space=pltpu.VMEM),
        out_shape=jax.ShapeDtypeStruct((blk_dev, share, feature), BF),
        scratch_shapes=[pltpu.VMEM((blk_dev, share, feature), F32)],
        cost_estimate=pl.CostEstimate(flops=500_000, bytes_accessed=1_000_000, transcendentals=0),
    )(asked, returned)


def by_ctx(move):
    return [(y * NZ + z, move(y) * NZ + z) for y in range(NY) for z in range(NZ)]


def by_head(move):
    return [(x * NC + c, move(x, c)) for x in range(NX) for c in range(NC)]


def to_x(k):
    return by_head(lambda x, c: (x + k) % NX * NC + c)


def from_x(k):
    return by_head(lambda x, c: (x - k) % NX * NC + c)


OTHER_CORE = by_head(lambda x, c: x * NC + 1 - c)


def body(latent_cache, queries, selected, block_home, w_uv, out_grad):
    owners = NY * NZ
    blk_dev, block_len, feature = latent_cache.shape
    latent = w_uv.shape[1]
    total = block_home.shape[0]
    nq, heads, _ = queries.shape
    share = block_len // (NX * NC)
    head_at = lax.axis_index("head")
    y_at = lax.axis_index("ctx").astype(jnp.int32) // NZ

    flat = selected.reshape(-1)
    flat_home = jnp.sum(
        jnp.where(flat[:, None] == jnp.arange(total)[None, :], block_home[None, :], 0), axis=1
    )
    request = wanted(selected.T, block_home, owners, blk_dev)
    asked = lax.all_to_all(request, "ctx", split_axis=0, concat_axis=0, tiled=True)

    q_t = jnp.transpose(queries, (1, 2, 0))
    og_heads = jnp.swapaxes(out_grad, 0, 1)
    mine = lax.dynamic_slice_in_dim(latent_cache, head_at * share, share, axis=1)
    asked, og_heads, mine = lax.optimization_barrier((asked, og_heads, mine))
    asked = asked.reshape(-1)

    outgoing = mine[jnp.maximum(asked, 0)]
    arrived = lax.all_to_all(
        outgoing.reshape(owners, CAP, share, feature), "ctx", split_axis=0, concat_axis=0, tiled=True
    ).reshape(owners * CAP, share, feature)

    valid = (request >= 0).reshape(-1)
    count = jnp.arange(owners * CAP)
    place = jnp.sum((valid[None, :] & (count[None, :] < count[:, None])).astype(jnp.int32), axis=1)
    hit = valid[None, :] & (place[None, :] == jnp.arange(UNIQ)[:, None])
    source = jnp.sum(jnp.where(hit, count[None, :], 0), axis=1)
    slot_home = (jnp.arange(owners)[:, None] * blk_dev + jnp.maximum(request, 0)).reshape(-1)
    pool_home = jnp.sum(jnp.where(hit, slot_home[None, :], 0), axis=1)
    chosen = jnp.max(
        (flat_home.reshape(nq, -1)[:, :, None] == pool_home[None, None, :]).astype(jnp.int32), axis=1
    )
    spot = jnp.minimum(place, UNIQ - 1)

    bias = jnp.where(chosen > 0, 0.0, OUTSIDE).astype(BF).T
    d_latent = jnp.einsum(
        "hcv,hqv->hcq", w_uv, og_heads, preferred_element_type=F32
    ).astype(BF)
    arrived, bias, d_latent, source, spot = lax.optimization_barrier(
        (arrived, bias, d_latent, source, spot)
    )

    own = arrived[source].reshape(UNIQ * share, feature)
    parts = [own] + [lax.ppermute(own, "head", from_x(k)) for k in range(1, NX)]
    parts = parts + [lax.ppermute(part, "head", OTHER_CORE) for part in parts]

    ds, out, keys, own_a, next_a, send_a, own_b, next_b, send_b, near, *far = forward(
        y_at.reshape(1), parts, bias, q_t, d_latent, og_heads
    )

    flip, turn = by_ctx(lambda y: y ^ 1), by_ctx(lambda y: y ^ 3)
    got_a = lax.ppermute(send_a, "ctx", flip)
    got_b = lax.ppermute(send_b, "ctx", turn)

    far_in = [lax.ppermute(part, "head", OTHER_CORE) for part in far]
    size = UNIQ * share
    quarter = [near[k * size:(k + 1) * size] + far_in[k] for k in range(NX)]
    leaving = [part.astype(BF) for part in quarter[1:]]
    ahead = [lax.ppermute(part, "head", to_x(k + 1)) for k, part in enumerate(leaving)]

    ds, out, _, own_quarter = lax.optimization_barrier((ds, out, leaving, quarter[0]))
    d_query, out_heads = rest(ds, keys, out, w_uv, feature)
    ahead, got_a, got_b, d_query, out_heads = lax.optimization_barrier(
        (ahead, got_a, got_b, d_query, out_heads)
    )

    pass_a = (next_a + got_a[1].astype(F32)).astype(BF)
    pass_b = (next_b + got_b[1].astype(F32)).astype(BF)
    pass_a, pass_b = lax.optimization_barrier((pass_a, pass_b))
    last_a = lax.ppermute(pass_a, "ctx", turn)
    last_b = lax.ppermute(pass_b, "ctx", flip)

    ahead, own_quarter, out_heads, _, _ = lax.optimization_barrier(
        (ahead, own_quarter, out_heads, pass_a, pass_b)
    )
    summed = own_quarter
    for part in ahead:
        summed = summed + part.astype(F32)
    outbound = summed.astype(BF).reshape(UNIQ, share, feature)[spot]
    head_out = jnp.swapaxes(out_heads, 0, 1)
    outbound, head_out, last_a, last_b = lax.optimization_barrier(
        (outbound, head_out, last_a, last_b)
    )
    returned = lax.all_to_all(
        outbound.reshape(owners, CAP, share, feature), "ctx", split_axis=0, concat_axis=0, tiled=True
    ).reshape(owners * CAP, share, feature)

    column = jnp.concatenate(
        [
            own_a + got_a[0].astype(F32) + last_a.astype(F32),
            own_b + got_b[0].astype(F32) + last_b.astype(F32),
        ],
        axis=1,
    )
    groups = [[y * NZ + z for z in range(NZ)] for y in range(NY)]
    weight_grad = lax.psum_scatter(
        column.reshape((NZ * heads,) + column.shape[2:]), "ctx", scatter_dimension=0,
        axis_index_groups=groups, tiled=True,
    ).astype(BF)

    cache_grad = settle(asked, returned, blk_dev)
    return (
        head_out, jnp.transpose(d_query, (2, 0, 1)), cache_grad, weight_grad
    )


def solution(mesh):
    in_specs = (
        P("ctx", None, None),
        P("ctx", "head", None),
        P("ctx", None),
        P(),
        P("head", None, None),
        P("ctx", "head", None),
    )
    out_specs = (
        P("ctx", "head", None),
        P("ctx", "head", None),
        P("ctx", "head", None),
        P("head", "ctx", None),
    )
    return jax.shard_map(body, mesh=mesh, in_specs=in_specs, out_specs=out_specs, check_vma=False)
```

```python
import jax
import jax.numpy as jnp
from jax import lax
from jax.experimental import pallas as pl
from jax.experimental.layout import Layout, with_layout_constraint
from jax.experimental.pallas import tpu as pltpu
from jax.sharding import PartitionSpec as P

NY, NZ, NX, NC = 4, 8, 4, 2
UNIQ = 16
CAP = 2
OUTSIDE = -1.0e6
TILE = 4
SUB = 2
CHUNK = 256
POOL_COLS = 512
FORWARD_VMEM = 56 * 1024 * 1024
REST_VMEM = 56 * 1024 * 1024

softmax_scale = 192.0 ** (-0.5)
LOG2E = 1.4426950408889634

BF = jnp.bfloat16
F32 = jnp.float32


def dot(a, b, ca, cb):
    return lax.dot_general(a, b, (((ca,), (cb,)), ((), ())), preferred_element_type=F32)


def forward_kernel(
    at_ref, k0_ref, k1_ref, k2_ref, k3_ref, k4_ref, k5_ref, k6_ref, k7_ref, bias_ref, qt_ref,
    dlt_ref, og_ref, ds_ref, out_ref, keys_ref, own_a_ref, next_a_ref, send_a_ref,
    own_b_ref, next_b_ref, send_b_ref, near_ref, f0_ref, f1_ref, f2_ref, f3_ref,
    values_t, pieces, low_ref,
):
    step = pl.program_id(0)
    tile, nq, _ = og_ref.shape
    wide = keys_ref.shape[1]
    rows, feature = keys_ref.shape[0], k0_ref.shape[1]
    latent = dlt_ref.shape[1]
    part = k0_ref.shape[0]
    group = part // UNIQ
    half = pl.num_programs(0) // 2
    pool_refs = (near_ref, f0_ref, f1_ref, f2_ref, f3_ref)

    @pl.when(step == 0)
    def _():
        for at, ref in enumerate((k0_ref, k1_ref, k2_ref, k3_ref, k4_ref, k5_ref, k6_ref, k7_ref)):
            keys_ref[at * part:(at + 1) * part, :feature] = ref[...]
        owner = (lax.broadcasted_iota(jnp.int32, (rows, wide - feature), 0) // group) % UNIQ
        lane = lax.broadcasted_iota(jnp.int32, (rows, wide - feature), 1)
        keys_ref[:, feature:] = (owner == lane).astype(F32).astype(BF)
        values_t[...] = keys_ref[:, :latent].T
        for ref in pool_refs:
            ref[...] = jnp.zeros_like(ref)

    per = min(SUB, tile)
    sub = per * nq
    rest = jnp.zeros((wide - feature - UNIQ, sub), BF)
    bias = jnp.concatenate([bias_ref[...]] * per, axis=1)

    def scored(j):
        q = jnp.concatenate([qt_ref[j * per + t] for t in range(per)], axis=1)
        return jnp.concatenate([q, bias, rest], axis=0)

    def carried(j):
        return jnp.concatenate([dlt_ref[j * per + t] for t in range(per)], axis=1)

    cols = [slice(at, at + sub) for at in range(0, tile * nq, sub)]
    rate = softmax_scale * LOG2E
    outs, qs, dls = [], [], []
    chunks = [slice(k, k + CHUNK) for k in range(0, rows, CHUNK)]
    def top_of(s):
        t = s[0].max(axis=0, keepdims=True)
        for x in s[1:]:
            t = jnp.maximum(t, x.max(axis=0, keepdims=True))
        return t * rate
    n = len(cols)
    ss, dd, pp = [None] * n, [None] * n, [None] * n
    for j in range(n + 1):
        if j < n:
            ss[j], dd[j] = [], []
            q, dl = scored(j), carried(j)
            qs.append(q)
            dls.append(dl)
        if j > 0:
            pp[j - 1], total, inner = [], 0.0, 0.0
            top = top_of(ss[j - 1])
        for ki, k in enumerate(chunks):
            if j < n:
                ss[j].append(dot(keys_ref[k], q, 1, 0))
            if j > 0:
                p = jnp.exp2(ss[j - 1][ki] * rate - top)
                pp[j - 1].append(p)
                total = total + p.sum(axis=0, keepdims=True)
                inner = inner + (p * dd[j - 1][ki]).sum(axis=0, keepdims=True)
        if j > 0:
            inv = 1.0 / total
            inner = inner * inv
            scaled = inv * softmax_scale
        for ki, k in enumerate(chunks):
            if j < n:
                dd[j].append(dot(keys_ref[k, :latent], dl, 1, 0))
            if j > 0:
                p = pp[j - 1][ki]
                low_ref[k, cols[j - 1]] = (p * inv).astype(BF)
                ds_ref[k, cols[j - 1]] = (p * scaled * (dd[j - 1][ki] - inner)).astype(BF)
        if j > 0:
            out = dot(values_t[...], low_ref[:, cols[j - 1]], 1, 0).astype(BF)
            for t in range(per):
                out_ref[(j - 1) * per + t] = out[:, t * nq:(t + 1) * nq]
            outs.append(out)
    depth = min(POOL_COLS, tile * nq)
    for lo in range(0, tile * nq, depth):
        span = slice(lo, lo + depth)
        here = range(lo // sub, (lo + depth) // sub)
        q = jnp.concatenate([qs[j] for j in here], axis=1)
        dl = jnp.concatenate([dls[j] for j in here], axis=1)
        for k in chunks:
            main = dot(ds_ref[k, span], q[:latent], 1, 1) + dot(low_ref[k, span], dl, 1, 1)
            side = dot(ds_ref[k, span], q[latent:feature], 1, 1)
            at = k.start
            for ref in pool_refs:
                n = ref.shape[0]
                if 0 <= at < n:
                    m = min(n - at, k.stop - k.start)
                    ref[at:at + m, :latent] += main[:m]
                    ref[at:at + m, latent:] += side[:m]
                    main, side, at = main[m:], side[m:], at + m
                    if main.shape[0] == 0:
                        break
                at -= n
    y, z = at_ref[0], at_ref[1]
    for t in range(tile):
        at = t * nq % sub
        wt = dot(outs[t * nq // sub][:, at:at + nq], og_ref[t], 1, 0)
        wt = wt.reshape(NY, NZ, latent // (NY * NZ), wt.shape[1])
        for part_y in range(NY):
            for part_z in range(NZ):
                pieces[part_y ^ y, lax.rem(part_z - z + NZ, NZ), t] = wt[part_y, part_z]

    @pl.when(step < half)
    def _():
        own_a_ref[...] = pieces[0]
        next_a_ref[...] = pieces[3]
        send_a_ref[0] = pieces[1].astype(BF)
        send_a_ref[1] = pieces[2].astype(BF)

    @pl.when(step >= half)
    def _():
        own_b_ref[...] = pieces[0]
        next_b_ref[...] = pieces[1]
        send_b_ref[0] = pieces[3].astype(BF)
        send_b_ref[1] = pieces[2].astype(BF)


def forward(at, parts, bias, qt, dlt, og):
    heads, nq, vd = og.shape
    latent = dlt.shape[1]
    part, feature = parts[0].shape
    wide = (feature + UNIQ + 127) // 128 * 128
    rows = len(parts) * part
    tile = TILE
    steps = heads // tile
    per = steps // 2
    sub = latent // (NY * NZ)
    whole = lambda *shape: pl.BlockSpec(shape, lambda i: (0,) * len(shape))
    cols = lambda n: pl.BlockSpec((n, tile * nq), lambda i: (0, i))
    heads_of = lambda *shape: pl.BlockSpec((tile,) + shape, lambda i: (i, 0, 0))
    at_a = lambda i: jnp.minimum(i, per - 1)
    at_b = lambda i: jnp.maximum(i - per, 0)

    def pieces_at(at):
        one = pl.BlockSpec((NZ, tile, sub, vd), lambda i: (0, at(i), 0, 0))
        two = pl.BlockSpec((2, NZ, tile, sub, vd), lambda i: (0, 0, at(i), 0, 0))
        return [one, one, two]

    sizes = [rows // 2] + [part] * NX
    shape = jax.ShapeDtypeStruct
    piece_shapes = [
        shape((NZ, heads // 2, sub, vd), F32), shape((NZ, heads // 2, sub, vd), F32),
        shape((2, NZ, heads // 2, sub, vd), BF),
    ]
    return pl.pallas_call(
        forward_kernel,
        grid=(steps,),
        in_specs=[pl.BlockSpec(memory_space=pltpu.SMEM)]
        + [whole(part, feature)] * len(parts)
        + [whole(UNIQ, nq), heads_of(feature, nq), heads_of(latent, nq),
           heads_of(nq, vd)],
        out_specs=[cols(rows), heads_of(latent, nq), whole(rows, wide)]
        + pieces_at(at_a) + pieces_at(at_b) + [whole(n, feature) for n in sizes],
        out_shape=[
            shape((rows, heads * nq), BF),
            shape((heads, latent, nq), BF), shape((rows, wide), BF),
        ] + piece_shapes * 2 + [shape((n, feature), F32) for n in sizes],
        scratch_shapes=[
            pltpu.VMEM((latent, rows), BF), pltpu.VMEM((NY, NZ, tile, sub, vd), F32),
            pltpu.VMEM((rows, tile * nq), BF),
        ],
        compiler_params=pltpu.CompilerParams(vmem_limit_bytes=FORWARD_VMEM),
        cost_estimate=pl.CostEstimate(
            flops=4 * heads * nq * rows * (wide + 2 * latent), bytes_accessed=16_000_000,
            transcendentals=heads * nq * rows,
        ),
    )(at, *parts, bias, qt, dlt, og)


def rest_kernel(ds_ref, keys_ref, out_ref, w_ref, dq_ref, ho_ref):
    tile, feature, nq = dq_ref.shape
    dq = dot(keys_ref[...], ds_ref[...], 0, 0)[:feature].astype(BF)
    for t in range(tile):
        dq_ref[t] = dq[:, t * nq:(t + 1) * nq]
        ho_ref[t] = dot(out_ref[t], w_ref[t], 0, 0).astype(BF)


def rest(ds, keys, out, w, feature):
    heads, latent, vd = w.shape
    rows, wide = keys.shape
    nq = out.shape[2]
    tile = TILE
    heads_of = lambda *shape: pl.BlockSpec((tile,) + shape, lambda i: (i, 0, 0))
    return pl.pallas_call(
        rest_kernel,
        grid=(heads // tile,),
        in_specs=[pl.BlockSpec((rows, tile * nq), lambda i: (0, i)),
                  pl.BlockSpec((rows, wide), lambda i: (0, 0)), heads_of(latent, nq),
                  heads_of(latent, vd)],
        out_specs=[heads_of(feature, nq), heads_of(nq, vd)],
        out_shape=[jax.ShapeDtypeStruct((heads, feature, nq), BF),
                   jax.ShapeDtypeStruct((heads, nq, vd), BF)],
        compiler_params=pltpu.CompilerParams(vmem_limit_bytes=REST_VMEM),
        cost_estimate=pl.CostEstimate(
            flops=1_000_000, bytes_accessed=100_000, transcendentals=0
        ),
    )(ds, keys, out, w)


def wanted_kernel(selected_ref, home_ref, out_ref):
    owners = out_ref.shape[0]
    blk_dev = home_ref.shape[0] * home_ref.shape[1] // owners
    names = selected_ref[...].T
    lane = lax.broadcasted_iota(jnp.int32, (names.shape[0], home_ref.shape[1]), 1)
    owner = lax.broadcasted_iota(jnp.int32, (owners, home_ref.shape[1]), 0)
    first = jnp.full(owner.shape, blk_dev, jnp.int32)
    last = jnp.full(owner.shape, -1, jnp.int32)
    for row in range(home_ref.shape[0]):
        named = jnp.zeros(lane.shape, jnp.int32)
        for k in range(names.shape[1]):
            named = jnp.where(names[:, k:k + 1] == lane + row * lane.shape[1], 1, named)
        named = jnp.max(named, axis=0, keepdims=True)
        home = home_ref[row:row + 1, :]
        here = (named > 0) & (lax.div(home, blk_dev) == owner)
        slot = lax.rem(home, blk_dev)
        first = jnp.minimum(first, jnp.where(here, slot, blk_dev))
        last = jnp.maximum(last, jnp.where(here, slot, -1))
    first = jnp.min(first, axis=1, keepdims=True)
    last = jnp.max(last, axis=1, keepdims=True)
    column = lax.broadcasted_iota(jnp.int32, out_ref.shape, 1)
    second = jnp.where(last > first, last, -1)
    out_ref[...] = jnp.where(column == 0, jnp.where(first < blk_dev, first, -1), second)


def wanted(selected_t, block_home, owners, blk_dev):
    vm = pl.BlockSpec(memory_space=pltpu.VMEM)
    return pl.pallas_call(
        wanted_kernel,
        in_specs=[vm, vm],
        out_specs=vm,
        out_shape=jax.ShapeDtypeStruct((owners, CAP), jnp.int32),
        cost_estimate=pl.CostEstimate(flops=3_000_000, bytes_accessed=10_000, transcendentals=0),
    )(selected_t, block_home.reshape(-1, 128))


def settle_kernel(asked_ref, returned_ref, out_ref, total):
    total[...] = jnp.zeros_like(total)

    def add(at, carry):
        slot = asked_ref[at]

        @pl.when(slot >= 0)
        def _():
            total[slot] += returned_ref[at].astype(F32)

        return carry

    lax.fori_loop(0, returned_ref.shape[0], add, 0)
    out_ref[...] = total[...].astype(BF)


def settle(asked, returned, blk_dev):
    _, share, feature = returned.shape
    return pl.pallas_call(
        settle_kernel,
        in_specs=[pl.BlockSpec(memory_space=pltpu.SMEM), pl.BlockSpec(memory_space=pltpu.VMEM)],
        out_specs=pl.BlockSpec(memory_space=pltpu.VMEM),
        out_shape=jax.ShapeDtypeStruct((blk_dev, share, feature), BF),
        scratch_shapes=[pltpu.VMEM((blk_dev, share, feature), F32)],
        cost_estimate=pl.CostEstimate(flops=500_000, bytes_accessed=1_000_000, transcendentals=0),
    )(asked, returned)


def by_ctx(move):
    return [(y * NZ + z, move(y) * NZ + z) for y in range(NY) for z in range(NZ)]


def to_z(k):
    return [(y * NZ + z, y * NZ + (z + k) % NZ) for y in range(NY) for z in range(NZ)]


def by_head(move):
    return [(x * NC + c, move(x, c)) for x in range(NX) for c in range(NC)]


def to_x(k):
    return by_head(lambda x, c: (x + k) % NX * NC + c)


def from_x(k):
    return by_head(lambda x, c: (x - k) % NX * NC + c)


OTHER_CORE = by_head(lambda x, c: x * NC + 1 - c)


def body(latent_cache, queries, selected, block_home, w_uv, out_grad):
    owners = NY * NZ
    blk_dev, block_len, feature = latent_cache.shape
    latent = w_uv.shape[1]
    total = block_home.shape[0]
    nq, heads, _ = queries.shape
    share = block_len // (NX * NC)
    head_at = lax.axis_index("head")
    ctx_at = lax.axis_index("ctx").astype(jnp.int32)

    flat = selected.reshape(-1)
    flat_home = jnp.sum(
        jnp.where(flat[:, None] == jnp.arange(total)[None, :], block_home[None, :], 0), axis=1
    )
    request = wanted(selected.T, block_home, owners, blk_dev)
    asked = lax.all_to_all(request, "ctx", split_axis=0, concat_axis=0, tiled=True)

    q_t = jnp.transpose(queries, (1, 2, 0))
    og_heads = jnp.swapaxes(out_grad, 0, 1)
    mine = lax.dynamic_slice_in_dim(latent_cache, head_at * share, share, axis=1)
    asked, og_heads, mine = lax.optimization_barrier((asked, og_heads, mine))
    asked = asked.reshape(-1)

    outgoing = mine[jnp.maximum(asked, 0)]
    arrived = lax.all_to_all(
        outgoing.reshape(owners, CAP, share, feature), "ctx", split_axis=0, concat_axis=0, tiled=True
    ).reshape(owners * CAP, share, feature)

    valid = (request >= 0).reshape(-1)
    count = jnp.arange(owners * CAP)
    place = jnp.sum((valid[None, :] & (count[None, :] < count[:, None])).astype(jnp.int32), axis=1)
    hit = valid[None, :] & (place[None, :] == jnp.arange(UNIQ)[:, None])
    source = jnp.sum(jnp.where(hit, count[None, :], 0), axis=1)
    slot_home = (jnp.arange(owners)[:, None] * blk_dev + jnp.maximum(request, 0)).reshape(-1)
    pool_home = jnp.sum(jnp.where(hit, slot_home[None, :], 0), axis=1)
    chosen = jnp.max(
        (flat_home.reshape(nq, -1)[:, :, None] == pool_home[None, None, :]).astype(jnp.int32), axis=1
    )
    spot = jnp.minimum(place, UNIQ - 1)

    bias = jnp.where(chosen > 0, 0.0, OUTSIDE).astype(BF).T
    d_latent = jnp.einsum(
        "hcv,hqv->hcq", w_uv, og_heads, preferred_element_type=F32
    ).astype(BF)
    arrived, bias, d_latent, source, spot = lax.optimization_barrier(
        (arrived, bias, d_latent, source, spot)
    )

    own = arrived[source].reshape(UNIQ * share, feature)
    parts = [own] + [lax.ppermute(own, "head", from_x(k)) for k in range(1, NX)]
    parts = parts + [lax.ppermute(part, "head", OTHER_CORE) for part in parts]

    ds, out, keys, own_a, next_a, send_a, own_b, next_b, send_b, near, *far = forward(
        jnp.stack([ctx_at // NZ, ctx_at % NZ]), parts, bias, q_t, d_latent, og_heads
    )

    flip, turn = by_ctx(lambda y: y ^ 1), by_ctx(lambda y: y ^ 3)
    got_a = lax.ppermute(send_a, "ctx", flip)
    got_b = lax.ppermute(send_b, "ctx", turn)

    far_in = [lax.ppermute(part, "head", OTHER_CORE) for part in far]
    size = UNIQ * share
    quarter = [near[k * size:(k + 1) * size] + far_in[k] for k in range(NX)]
    leaving = [part.astype(BF) for part in quarter[1:]]
    ahead = [lax.ppermute(part, "head", to_x(k + 1)) for k, part in enumerate(leaving)]

    ds, out, _, own_quarter = lax.optimization_barrier((ds, out, leaving, quarter[0]))
    d_query, out_heads = rest(ds, keys, out, w_uv, feature)
    ahead, got_a, got_b, d_query, out_heads = lax.optimization_barrier(
        (ahead, got_a, got_b, d_query, out_heads)
    )

    pass_a = (next_a + got_a[1].astype(F32)).astype(BF)
    pass_b = (next_b + got_b[1].astype(F32)).astype(BF)
    pass_a, pass_b = lax.optimization_barrier((pass_a, pass_b))
    last_a = lax.ppermute(pass_a, "ctx", turn)
    last_b = lax.ppermute(pass_b, "ctx", flip)

    ahead, own_quarter, out_heads, _, _ = lax.optimization_barrier(
        (ahead, own_quarter, out_heads, pass_a, pass_b)
    )
    summed = own_quarter
    for part in ahead:
        summed = summed + part.astype(F32)
    outbound = summed.astype(BF).reshape(UNIQ, share, feature)[spot]
    returned = lax.all_to_all(
        outbound.reshape(owners, CAP, share, feature), "ctx", split_axis=0, concat_axis=0, tiled=True
    ).reshape(owners * CAP, share, feature)

    head_out = with_layout_constraint(
        jnp.swapaxes(out_heads, 0, 1), Layout(major_to_minor=(0, 1, 2))
    )
    last_a, last_b, head_out, _ = lax.optimization_barrier((last_a, last_b, head_out, outbound))
    column = jnp.concatenate(
        [
            own_a + got_a[0].astype(F32) + last_a.astype(F32),
            own_b + got_b[0].astype(F32) + last_b.astype(F32),
        ],
        axis=1,
    )
    weight_sum = column[0]
    for k in (4, 3, 5, 2, 6, 1, 7):
        weight_sum = weight_sum + lax.ppermute(column[k].astype(BF), "ctx", to_z(k)).astype(F32)
    weight_grad = weight_sum.astype(BF)

    cache_grad = settle(asked, returned, blk_dev)
    return (
        head_out, jnp.transpose(d_query, (2, 0, 1)), cache_grad, weight_grad
    )


def solution(mesh):
    in_specs = (
        P("ctx", None, None),
        P("ctx", "head", None),
        P("ctx", None),
        P(),
        P("head", None, None),
        P("ctx", "head", None),
    )
    out_specs = (
        P("ctx", "head", None),
        P("ctx", "head", None),
        P("ctx", "head", None),
        P("head", "ctx", None),
    )
    return jax.shard_map(body, mesh=mesh, in_specs=in_specs, out_specs=out_specs, check_vma=False)
```

```python
import jax
import jax.numpy as jnp
from jax import lax
from jax.experimental import pallas as pl
from jax.experimental.layout import Layout, with_layout_constraint
from jax.experimental.pallas import tpu as pltpu
from jax.sharding import PartitionSpec as P

NY, NZ, NX, NC = 4, 8, 4, 2
UNIQ = 16
CAP = 2
OUTSIDE = -1.0e6
TILE = 4
SUB = 2
CHUNK = 256
POOL_COLS = 512
FORWARD_VMEM = 56 * 1024 * 1024
REST_VMEM = 56 * 1024 * 1024

softmax_scale = 192.0 ** (-0.5)
LOG2E = 1.4426950408889634

BF = jnp.bfloat16
F32 = jnp.float32


def dot(a, b, ca, cb):
    return lax.dot_general(a, b, (((ca,), (cb,)), ((), ())), preferred_element_type=F32)


def forward_kernel(
    at_ref, k0_ref, k1_ref, k2_ref, k3_ref, k4_ref, k5_ref, k6_ref, k7_ref, bias_ref, qt_ref,
    dlt_ref, og_ref, ds_ref, out_ref, keys_ref, own_a_ref, next_a_ref, send_a_ref,
    own_b_ref, next_b_ref, send_b_ref, near_ref, f0_ref, f1_ref, f2_ref, f3_ref,
    values_t, pieces, low_ref,
):
    step = pl.program_id(0)
    tile, nq, _ = og_ref.shape
    wide = keys_ref.shape[1]
    rows, feature = keys_ref.shape[0], k0_ref.shape[1]
    latent = dlt_ref.shape[1]
    part = k0_ref.shape[0]
    group = part // UNIQ
    half = pl.num_programs(0) // 2
    pool_refs = (near_ref, f0_ref, f1_ref, f2_ref, f3_ref)

    @pl.when(step == 0)
    def _():
        for at, ref in enumerate((k0_ref, k1_ref, k2_ref, k3_ref, k4_ref, k5_ref, k6_ref, k7_ref)):
            keys_ref[at * part:(at + 1) * part, :feature] = ref[...]
        owner = (lax.broadcasted_iota(jnp.int32, (rows, wide - feature), 0) // group) % UNIQ
        lane = lax.broadcasted_iota(jnp.int32, (rows, wide - feature), 1)
        keys_ref[:, feature:] = (owner == lane).astype(F32).astype(BF)
        values_t[...] = keys_ref[:, :latent].T
        for ref in pool_refs:
            ref[...] = jnp.zeros_like(ref)

    per = min(SUB, tile)
    sub = per * nq
    rest = jnp.zeros((wide - feature - UNIQ, sub), BF)
    bias = jnp.concatenate([bias_ref[...]] * per, axis=1)

    def scored(j):
        q = jnp.concatenate([qt_ref[j * per + t] for t in range(per)], axis=1)
        return jnp.concatenate([q, bias, rest], axis=0)

    def carried(j):
        return jnp.concatenate([dlt_ref[j * per + t] for t in range(per)], axis=1)

    cols = [slice(at, at + sub) for at in range(0, tile * nq, sub)]
    rate = softmax_scale * LOG2E
    outs, qs, dls = [], [], []
    chunks = [slice(k, k + CHUNK) for k in range(0, rows, CHUNK)]
    def top_of(s):
        t = s[0].max(axis=0, keepdims=True)
        for x in s[1:]:
            t = jnp.maximum(t, x.max(axis=0, keepdims=True))
        return t * rate
    n = len(cols)
    ss, dd, pp = [None] * n, [None] * n, [None] * n
    for j in range(n + 1):
        if j < n:
            ss[j], dd[j] = [], []
            q, dl = scored(j), carried(j)
            qs.append(q)
            dls.append(dl)
        if j > 0:
            pp[j - 1], total, inner = [], 0.0, 0.0
            top = top_of(ss[j - 1])
        for ki, k in enumerate(chunks):
            if j < n:
                ss[j].append(dot(keys_ref[k], q, 1, 0))
            if j > 0:
                p = jnp.exp2(ss[j - 1][ki] * rate - top)
                pp[j - 1].append(p)
                total = total + p.sum(axis=0, keepdims=True)
                inner = inner + (p * dd[j - 1][ki]).sum(axis=0, keepdims=True)
        if j > 0:
            inv = 1.0 / total
            inner = inner * inv
            scaled = inv * softmax_scale
        for ki, k in enumerate(chunks):
            if j < n:
                dd[j].append(dot(keys_ref[k, :latent], dl, 1, 0))
            if j > 0:
                p = pp[j - 1][ki]
                low_ref[k, cols[j - 1]] = (p * inv).astype(BF)
                ds_ref[k, cols[j - 1]] = (p * scaled * (dd[j - 1][ki] - inner)).astype(BF)
        if j > 0:
            out = dot(values_t[...], low_ref[:, cols[j - 1]], 1, 0).astype(BF)
            for t in range(per):
                out_ref[(j - 1) * per + t] = out[:, t * nq:(t + 1) * nq]
            outs.append(out)
    depth = min(POOL_COLS, tile * nq)
    for lo in range(0, tile * nq, depth):
        span = slice(lo, lo + depth)
        here = range(lo // sub, (lo + depth) // sub)
        q = jnp.concatenate([qs[j] for j in here], axis=1)
        dl = jnp.concatenate([dls[j] for j in here], axis=1)
        for k in chunks:
            main = dot(ds_ref[k, span], q[:latent], 1, 1) + dot(low_ref[k, span], dl, 1, 1)
            side = dot(ds_ref[k, span], q[latent:feature], 1, 1)
            at = k.start
            for ref in pool_refs:
                n = ref.shape[0]
                if 0 <= at < n:
                    m = min(n - at, k.stop - k.start)
                    ref[at:at + m, :latent] += main[:m]
                    ref[at:at + m, latent:] += side[:m]
                    main, side, at = main[m:], side[m:], at + m
                    if main.shape[0] == 0:
                        break
                at -= n
    y, z = at_ref[0], at_ref[1]
    for t in range(tile):
        at = t * nq % sub
        wt = dot(outs[t * nq // sub][:, at:at + nq], og_ref[t], 1, 0)
        wt = wt.reshape(NY, NZ, latent // (NY * NZ), wt.shape[1])
        for part_y in range(NY):
            for part_z in range(NZ):
                pieces[part_y ^ y, lax.rem(part_z - z + NZ, NZ), t] = wt[part_y, part_z]

    @pl.when(step < half)
    def _():
        own_a_ref[...] = pieces[0]
        next_a_ref[...] = pieces[3]
        send_a_ref[0] = pieces[1].astype(BF)
        send_a_ref[1] = pieces[2].astype(BF)

    @pl.when(step >= half)
    def _():
        own_b_ref[...] = pieces[0]
        next_b_ref[...] = pieces[1]
        send_b_ref[0] = pieces[3].astype(BF)
        send_b_ref[1] = pieces[2].astype(BF)


def forward(at, parts, bias, qt, dlt, og):
    heads, nq, vd = og.shape
    latent = dlt.shape[1]
    part, feature = parts[0].shape
    wide = (feature + UNIQ + 127) // 128 * 128
    rows = len(parts) * part
    tile = TILE
    steps = heads // tile
    per = steps // 2
    sub = latent // (NY * NZ)
    whole = lambda *shape: pl.BlockSpec(shape, lambda i: (0,) * len(shape))
    cols = lambda n: pl.BlockSpec((n, tile * nq), lambda i: (0, i))
    heads_of = lambda *shape: pl.BlockSpec((tile,) + shape, lambda i: (i, 0, 0))
    at_a = lambda i: jnp.minimum(i, per - 1)
    at_b = lambda i: jnp.maximum(i - per, 0)

    def pieces_at(at):
        one = pl.BlockSpec((NZ, tile, sub, vd), lambda i: (0, at(i), 0, 0))
        two = pl.BlockSpec((2, NZ, tile, sub, vd), lambda i: (0, 0, at(i), 0, 0))
        return [one, one, two]

    sizes = [rows // 2] + [part] * NX
    shape = jax.ShapeDtypeStruct
    piece_shapes = [
        shape((NZ, heads // 2, sub, vd), F32), shape((NZ, heads // 2, sub, vd), F32),
        shape((2, NZ, heads // 2, sub, vd), BF),
    ]
    return pl.pallas_call(
        forward_kernel,
        grid=(steps,),
        in_specs=[pl.BlockSpec(memory_space=pltpu.SMEM)]
        + [whole(part, feature)] * len(parts)
        + [whole(UNIQ, nq), heads_of(feature, nq), heads_of(latent, nq),
           heads_of(nq, vd)],
        out_specs=[cols(rows), heads_of(latent, nq), whole(rows, wide)]
        + pieces_at(at_a) + pieces_at(at_b) + [whole(n, feature) for n in sizes],
        out_shape=[
            shape((rows, heads * nq), BF),
            shape((heads, latent, nq), BF), shape((rows, wide), BF),
        ] + piece_shapes * 2 + [shape((n, feature), F32) for n in sizes],
        scratch_shapes=[
            pltpu.VMEM((latent, rows), BF), pltpu.VMEM((NY, NZ, tile, sub, vd), F32),
            pltpu.VMEM((rows, tile * nq), BF),
        ],
        compiler_params=pltpu.CompilerParams(vmem_limit_bytes=FORWARD_VMEM),
        cost_estimate=pl.CostEstimate(
            flops=4 * heads * nq * rows * (wide + 2 * latent), bytes_accessed=16_000_000,
            transcendentals=heads * nq * rows,
        ),
    )(at, *parts, bias, qt, dlt, og)


def rest_kernel(ds_ref, keys_ref, out_ref, w_ref, dq_ref, ho_ref):
    tile, feature, nq = dq_ref.shape
    dq = dot(keys_ref[...], ds_ref[...], 0, 0)[:feature].astype(BF)
    for t in range(tile):
        dq_ref[t] = dq[:, t * nq:(t + 1) * nq]
        ho_ref[t] = dot(out_ref[t], w_ref[t], 0, 0).astype(BF)


def rest(ds, keys, out, w, feature):
    heads, latent, vd = w.shape
    rows, wide = keys.shape
    nq = out.shape[2]
    tile = TILE
    heads_of = lambda *shape: pl.BlockSpec((tile,) + shape, lambda i: (i, 0, 0))
    return pl.pallas_call(
        rest_kernel,
        grid=(heads // tile,),
        in_specs=[pl.BlockSpec((rows, tile * nq), lambda i: (0, i)),
                  pl.BlockSpec((rows, wide), lambda i: (0, 0)), heads_of(latent, nq),
                  heads_of(latent, vd)],
        out_specs=[heads_of(feature, nq), heads_of(nq, vd)],
        out_shape=[jax.ShapeDtypeStruct((heads, feature, nq), BF),
                   jax.ShapeDtypeStruct((heads, nq, vd), BF)],
        compiler_params=pltpu.CompilerParams(vmem_limit_bytes=REST_VMEM),
        cost_estimate=pl.CostEstimate(
            flops=1_000_000, bytes_accessed=100_000, transcendentals=0
        ),
    )(ds, keys, out, w)


def wanted_kernel(selected_ref, home_ref, out_ref):
    owners = out_ref.shape[0]
    blk_dev = home_ref.shape[0] * home_ref.shape[1] // owners
    names = selected_ref[...].T
    lane = lax.broadcasted_iota(jnp.int32, (names.shape[0], home_ref.shape[1]), 1)
    owner = lax.broadcasted_iota(jnp.int32, (owners, home_ref.shape[1]), 0)
    first = jnp.full(owner.shape, blk_dev, jnp.int32)
    last = jnp.full(owner.shape, -1, jnp.int32)
    for row in range(home_ref.shape[0]):
        named = jnp.zeros(lane.shape, jnp.int32)
        for k in range(names.shape[1]):
            named = jnp.where(names[:, k:k + 1] == lane + row * lane.shape[1], 1, named)
        named = jnp.max(named, axis=0, keepdims=True)
        home = home_ref[row:row + 1, :]
        here = (named > 0) & (lax.div(home, blk_dev) == owner)
        slot = lax.rem(home, blk_dev)
        first = jnp.minimum(first, jnp.where(here, slot, blk_dev))
        last = jnp.maximum(last, jnp.where(here, slot, -1))
    first = jnp.min(first, axis=1, keepdims=True)
    last = jnp.max(last, axis=1, keepdims=True)
    column = lax.broadcasted_iota(jnp.int32, out_ref.shape, 1)
    second = jnp.where(last > first, last, -1)
    out_ref[...] = jnp.where(column == 0, jnp.where(first < blk_dev, first, -1), second)


def wanted(selected_t, block_home, owners, blk_dev):
    vm = pl.BlockSpec(memory_space=pltpu.VMEM)
    return pl.pallas_call(
        wanted_kernel,
        in_specs=[vm, vm],
        out_specs=vm,
        out_shape=jax.ShapeDtypeStruct((owners, CAP), jnp.int32),
        cost_estimate=pl.CostEstimate(flops=3_000_000, bytes_accessed=10_000, transcendentals=0),
    )(selected_t, block_home.reshape(-1, 128))


def settle_kernel(asked_ref, returned_ref, out_ref, total):
    total[...] = jnp.zeros_like(total)

    def add(at, carry):
        slot = asked_ref[at]

        @pl.when(slot >= 0)
        def _():
            total[slot] += returned_ref[at].astype(F32)

        return carry

    lax.fori_loop(0, returned_ref.shape[0], add, 0)
    out_ref[...] = total[...].astype(BF)


def settle(asked, returned, blk_dev):
    _, share, feature = returned.shape
    return pl.pallas_call(
        settle_kernel,
        in_specs=[pl.BlockSpec(memory_space=pltpu.SMEM), pl.BlockSpec(memory_space=pltpu.VMEM)],
        out_specs=pl.BlockSpec(memory_space=pltpu.VMEM),
        out_shape=jax.ShapeDtypeStruct((blk_dev, share, feature), BF),
        scratch_shapes=[pltpu.VMEM((blk_dev, share, feature), F32)],
        cost_estimate=pl.CostEstimate(flops=500_000, bytes_accessed=1_000_000, transcendentals=0),
    )(asked, returned)


def by_ctx(move):
    return [(y * NZ + z, move(y) * NZ + z) for y in range(NY) for z in range(NZ)]


def to_z(k):
    return [(y * NZ + z, y * NZ + (z + k) % NZ) for y in range(NY) for z in range(NZ)]


def by_head(move):
    return [(x * NC + c, move(x, c)) for x in range(NX) for c in range(NC)]


def to_x(k):
    return by_head(lambda x, c: (x + k) % NX * NC + c)


def from_x(k):
    return by_head(lambda x, c: (x - k) % NX * NC + c)


OTHER_CORE = by_head(lambda x, c: x * NC + 1 - c)


def body(latent_cache, queries, selected, block_home, w_uv, out_grad):
    owners = NY * NZ
    blk_dev, block_len, feature = latent_cache.shape
    latent = w_uv.shape[1]
    total = block_home.shape[0]
    nq, heads, _ = queries.shape
    share = block_len // (NX * NC)
    head_at = lax.axis_index("head")
    ctx_at = lax.axis_index("ctx").astype(jnp.int32)

    flat = selected.reshape(-1)
    flat_home = jnp.sum(
        jnp.where(flat[:, None] == jnp.arange(total)[None, :], block_home[None, :], 0), axis=1
    )
    request = wanted(selected.T, block_home, owners, blk_dev)
    asked = lax.all_to_all(request, "ctx", split_axis=0, concat_axis=0, tiled=True)

    q_t = jnp.transpose(queries, (1, 2, 0))
    og_heads = jnp.swapaxes(out_grad, 0, 1)
    mine = lax.dynamic_slice_in_dim(latent_cache, head_at * share, share, axis=1)
    asked, og_heads, mine = lax.optimization_barrier((asked, og_heads, mine))
    asked = asked.reshape(-1)

    outgoing = mine[jnp.maximum(asked, 0)]
    arrived = lax.all_to_all(
        outgoing.reshape(owners, CAP, share, feature), "ctx", split_axis=0, concat_axis=0, tiled=True
    ).reshape(owners * CAP, share, feature)

    valid = (request >= 0).reshape(-1)
    count = jnp.arange(owners * CAP)
    place = jnp.sum((valid[None, :] & (count[None, :] < count[:, None])).astype(jnp.int32), axis=1)
    hit = valid[None, :] & (place[None, :] == jnp.arange(UNIQ)[:, None])
    source = jnp.sum(jnp.where(hit, count[None, :], 0), axis=1)
    slot_home = (jnp.arange(owners)[:, None] * blk_dev + jnp.maximum(request, 0)).reshape(-1)
    pool_home = jnp.sum(jnp.where(hit, slot_home[None, :], 0), axis=1)
    chosen = jnp.max(
        (flat_home.reshape(nq, -1)[:, :, None] == pool_home[None, None, :]).astype(jnp.int32), axis=1
    )
    spot = jnp.minimum(place, UNIQ - 1)

    bias = jnp.where(chosen > 0, 0.0, OUTSIDE).astype(BF).T
    d_latent = jnp.einsum(
        "hcv,hqv->hcq", w_uv, og_heads, preferred_element_type=F32
    ).astype(BF)
    arrived, bias, d_latent, source, spot = lax.optimization_barrier(
        (arrived, bias, d_latent, source, spot)
    )

    own = arrived[source].reshape(UNIQ * share, feature)
    parts = [own] + [lax.ppermute(own, "head", from_x(k)) for k in range(1, NX)]
    parts = parts + [lax.ppermute(part, "head", OTHER_CORE) for part in parts]

    ds, out, keys, own_a, next_a, send_a, own_b, next_b, send_b, near, *far = forward(
        jnp.stack([ctx_at // NZ, ctx_at % NZ]), parts, bias, q_t, d_latent, og_heads
    )

    flip, turn = by_ctx(lambda y: y ^ 1), by_ctx(lambda y: y ^ 3)
    got_a = lax.ppermute(send_a, "ctx", flip)
    got_b = lax.ppermute(send_b, "ctx", turn)

    far_in = [lax.ppermute(part, "head", OTHER_CORE) for part in far]
    size = UNIQ * share
    quarter = [near[k * size:(k + 1) * size] + far_in[k] for k in range(NX)]
    leaving = [part.astype(BF) for part in quarter[1:]]
    ahead = [lax.ppermute(part, "head", to_x(k + 1)) for k, part in enumerate(leaving)]

    ds, out, _, own_quarter = lax.optimization_barrier((ds, out, leaving, quarter[0]))
    d_query, out_heads = rest(ds, keys, out, w_uv, feature)
    ahead, got_a, got_b, d_query, out_heads = lax.optimization_barrier(
        (ahead, got_a, got_b, d_query, out_heads)
    )

    pass_a = (next_a + got_a[1].astype(F32)).astype(BF)
    pass_b = (next_b + got_b[1].astype(F32)).astype(BF)
    pass_a, pass_b = lax.optimization_barrier((pass_a, pass_b))
    last_a = lax.ppermute(pass_a, "ctx", turn)
    last_b = lax.ppermute(pass_b, "ctx", flip)

    ahead, own_quarter, out_heads, _, _ = lax.optimization_barrier(
        (ahead, own_quarter, out_heads, pass_a, pass_b)
    )
    summed = own_quarter
    for part in ahead:
        summed = summed + part.astype(F32)
    outbound = summed.astype(BF).reshape(UNIQ, share, feature)[spot]
    returned = lax.all_to_all(
        outbound.reshape(owners, CAP, share, feature), "ctx", split_axis=0, concat_axis=0, tiled=True
    ).reshape(owners * CAP, share, feature)

    head_out = with_layout_constraint(
        jnp.swapaxes(out_heads, 0, 1), Layout(major_to_minor=(0, 1, 2))
    )
    last_a, last_b, head_out, _ = lax.optimization_barrier((last_a, last_b, head_out, outbound))
    column = jnp.concatenate(
        [
            own_a + got_a[0].astype(F32) + last_a.astype(F32),
            own_b + got_b[0].astype(F32) + last_b.astype(F32),
        ],
        axis=1,
    )
    along = [lax.ppermute(column[k].astype(BF), "ctx", to_z(k)) for k in (1, 6, 2, 5, 3, 4, 7)]
    cache_grad = settle(asked, returned, blk_dev)
    along, cache_grad = lax.optimization_barrier((along, cache_grad))
    weight_sum = column[0]
    for part in along:
        weight_sum = weight_sum + part.astype(F32)
    weight_grad = weight_sum.astype(BF)

    return (
        head_out, jnp.transpose(d_query, (2, 0, 1)), cache_grad, weight_grad
    )


def solution(mesh):
    in_specs = (
        P("ctx", None, None),
        P("ctx", "head", None),
        P("ctx", None),
        P(),
        P("head", None, None),
        P("ctx", "head", None),
    )
    out_specs = (
        P("ctx", "head", None),
        P("ctx", "head", None),
        P("ctx", "head", None),
        P("head", "ctx", None),
    )
    return jax.shard_map(body, mesh=mesh, in_specs=in_specs, out_specs=out_specs, check_vma=False)
```

```python
import jax
import jax.numpy as jnp
from jax import lax
from jax.experimental import pallas as pl
from jax.experimental.layout import Layout, with_layout_constraint
from jax.experimental.pallas import tpu as pltpu
from jax.sharding import PartitionSpec as P

NY, NZ, NX, NC = 4, 8, 4, 2
UNIQ = 16
CAP = 2
OUTSIDE = -1.0e6
TILE = 4
SUB = 2
CHUNK = 256
POOL_COLS = 512
FORWARD_VMEM = 56 * 1024 * 1024
REST_VMEM = 56 * 1024 * 1024

softmax_scale = 192.0 ** (-0.5)
LOG2E = 1.4426950408889634

BF = jnp.bfloat16
F32 = jnp.float32


def dot(a, b, ca, cb):
    return lax.dot_general(a, b, (((ca,), (cb,)), ((), ())), preferred_element_type=F32)


def forward_kernel(
    at_ref, k0_ref, k1_ref, k2_ref, k3_ref, k4_ref, k5_ref, k6_ref, k7_ref, bias_ref, qt_ref,
    dlt_ref, og_ref, ds_ref, out_ref, keys_ref, own_a_ref, next_a_ref, send_a_ref,
    own_b_ref, next_b_ref, send_b_ref, near_ref, f0_ref, f1_ref, f2_ref, f3_ref,
    values_t, pieces, low_ref,
):
    step = pl.program_id(0)
    tile, nq, _ = og_ref.shape
    wide = keys_ref.shape[1]
    rows, feature = keys_ref.shape[0], k0_ref.shape[1]
    latent = dlt_ref.shape[1]
    part = k0_ref.shape[0]
    group = part // UNIQ
    half = pl.num_programs(0) // 2
    pool_refs = (near_ref, f0_ref, f1_ref, f2_ref, f3_ref)

    @pl.when(step == 0)
    def _():
        for at, ref in enumerate((k0_ref, k1_ref, k2_ref, k3_ref, k4_ref, k5_ref, k6_ref, k7_ref)):
            keys_ref[at * part:(at + 1) * part, :feature] = ref[...]
        owner = (lax.broadcasted_iota(jnp.int32, (rows, wide - feature), 0) // group) % UNIQ
        lane = lax.broadcasted_iota(jnp.int32, (rows, wide - feature), 1)
        keys_ref[:, feature:] = (owner == lane).astype(F32).astype(BF)
        values_t[...] = keys_ref[:, :latent].T
        for ref in pool_refs:
            ref[...] = jnp.zeros_like(ref)

    per = min(SUB, tile)
    sub = per * nq
    rest = jnp.zeros((wide - feature - UNIQ, sub), BF)
    bias = jnp.concatenate([bias_ref[...]] * per, axis=1)

    def scored(j):
        q = jnp.concatenate([qt_ref[j * per + t] for t in range(per)], axis=1)
        return jnp.concatenate([q, bias, rest], axis=0)

    def carried(j):
        return jnp.concatenate([dlt_ref[j * per + t] for t in range(per)], axis=1)

    cols = [slice(at, at + sub) for at in range(0, tile * nq, sub)]
    rate = softmax_scale * LOG2E
    outs, qs, dls = [], [], []
    chunks = [slice(k, k + CHUNK) for k in range(0, rows, CHUNK)]
    def top_of(s):
        t = s[0].max(axis=0, keepdims=True)
        for x in s[1:]:
            t = jnp.maximum(t, x.max(axis=0, keepdims=True))
        return t * rate
    n = len(cols)
    ss, dd, pp = [None] * n, [None] * n, [None] * n
    for j in range(n + 1):
        if j < n:
            ss[j], dd[j] = [], []
            q, dl = scored(j), carried(j)
            qs.append(q)
            dls.append(dl)
        if j > 0:
            pp[j - 1], total, inner = [], 0.0, 0.0
            top = top_of(ss[j - 1])
        for ki, k in enumerate(chunks):
            if j < n:
                ss[j].append(dot(keys_ref[k], q, 1, 0))
            if j > 0:
                p = jnp.exp2(ss[j - 1][ki] * rate - top)
                pp[j - 1].append(p)
                total = total + p.sum(axis=0, keepdims=True)
                inner = inner + (p * dd[j - 1][ki]).sum(axis=0, keepdims=True)
        if j > 0:
            inv = 1.0 / total
            inner = inner * inv
            scaled = inv * softmax_scale
        for ki, k in enumerate(chunks):
            if j < n:
                dd[j].append(dot(keys_ref[k, :latent], dl, 1, 0))
            if j > 0:
                p = pp[j - 1][ki]
                low_ref[k, cols[j - 1]] = (p * inv).astype(BF)
                ds_ref[k, cols[j - 1]] = (p * scaled * (dd[j - 1][ki] - inner)).astype(BF)
        if j > 0:
            out = dot(values_t[...], low_ref[:, cols[j - 1]], 1, 0).astype(BF)
            for t in range(per):
                out_ref[(j - 1) * per + t] = out[:, t * nq:(t + 1) * nq]
            outs.append(out)
    depth = min(POOL_COLS, tile * nq)
    for lo in range(0, tile * nq, depth):
        span = slice(lo, lo + depth)
        here = range(lo // sub, (lo + depth) // sub)
        q = jnp.concatenate([qs[j] for j in here], axis=1)
        dl = jnp.concatenate([dls[j] for j in here], axis=1)
        for k in chunks:
            main = dot(ds_ref[k, span], q[:latent], 1, 1) + dot(low_ref[k, span], dl, 1, 1)
            side = dot(ds_ref[k, span], q[latent:feature], 1, 1)
            at = k.start
            for ref in pool_refs:
                n = ref.shape[0]
                if 0 <= at < n:
                    m = min(n - at, k.stop - k.start)
                    ref[at:at + m, :latent] += main[:m]
                    ref[at:at + m, latent:] += side[:m]
                    main, side, at = main[m:], side[m:], at + m
                    if main.shape[0] == 0:
                        break
                at -= n
    y, z = at_ref[0], at_ref[1]
    for t in range(tile):
        at = t * nq % sub
        wt = dot(outs[t * nq // sub][:, at:at + nq], og_ref[t], 1, 0)
        wt = wt.reshape(NY, NZ, latent // (NY * NZ), wt.shape[1])
        for part_y in range(NY):
            for part_z in range(NZ):
                pieces[part_y ^ y, lax.rem(part_z - z + NZ, NZ), t] = wt[part_y, part_z]

    @pl.when(step < half)
    def _():
        own_a_ref[...] = pieces[0]
        next_a_ref[...] = pieces[3]
        send_a_ref[0] = pieces[1].astype(BF)
        send_a_ref[1] = pieces[2].astype(BF)

    @pl.when(step >= half)
    def _():
        own_b_ref[...] = pieces[0]
        next_b_ref[...] = pieces[1]
        send_b_ref[0] = pieces[3].astype(BF)
        send_b_ref[1] = pieces[2].astype(BF)


def forward(at, parts, bias, qt, dlt, og):
    heads, nq, vd = og.shape
    latent = dlt.shape[1]
    part, feature = parts[0].shape
    wide = (feature + UNIQ + 127) // 128 * 128
    rows = len(parts) * part
    tile = TILE
    steps = heads // tile
    per = steps // 2
    sub = latent // (NY * NZ)
    whole = lambda *shape: pl.BlockSpec(shape, lambda i: (0,) * len(shape))
    cols = lambda n: pl.BlockSpec((n, tile * nq), lambda i: (0, i))
    heads_of = lambda *shape: pl.BlockSpec((tile,) + shape, lambda i: (i, 0, 0))
    at_a = lambda i: jnp.minimum(i, per - 1)
    at_b = lambda i: jnp.maximum(i - per, 0)

    def pieces_at(at):
        one = pl.BlockSpec((NZ, tile, sub, vd), lambda i: (0, at(i), 0, 0))
        two = pl.BlockSpec((2, NZ, tile, sub, vd), lambda i: (0, 0, at(i), 0, 0))
        return [one, one, two]

    sizes = [rows // 2] + [part] * NX
    shape = jax.ShapeDtypeStruct
    piece_shapes = [
        shape((NZ, heads // 2, sub, vd), F32), shape((NZ, heads // 2, sub, vd), F32),
        shape((2, NZ, heads // 2, sub, vd), BF),
    ]
    return pl.pallas_call(
        forward_kernel,
        grid=(steps,),
        in_specs=[pl.BlockSpec(memory_space=pltpu.SMEM)]
        + [whole(part, feature)] * len(parts)
        + [whole(UNIQ, nq), heads_of(feature, nq), heads_of(latent, nq),
           heads_of(nq, vd)],
        out_specs=[cols(rows), heads_of(latent, nq), whole(rows, wide)]
        + pieces_at(at_a) + pieces_at(at_b) + [whole(n, feature) for n in sizes],
        out_shape=[
            shape((rows, heads * nq), BF),
            shape((heads, latent, nq), BF), shape((rows, wide), BF),
        ] + piece_shapes * 2 + [shape((n, feature), F32) for n in sizes],
        scratch_shapes=[
            pltpu.VMEM((latent, rows), BF), pltpu.VMEM((NY, NZ, tile, sub, vd), F32),
            pltpu.VMEM((rows, tile * nq), BF),
        ],
        compiler_params=pltpu.CompilerParams(vmem_limit_bytes=FORWARD_VMEM),
        cost_estimate=pl.CostEstimate(
            flops=4 * heads * nq * rows * (wide + 2 * latent), bytes_accessed=16_000_000,
            transcendentals=heads * nq * rows,
        ),
    )(at, *parts, bias, qt, dlt, og)


def rest_kernel(ds_ref, keys_ref, out_ref, w_ref, dq_ref, ho_ref):
    tile, feature, nq = dq_ref.shape
    dq = dot(keys_ref[...], ds_ref[...], 0, 0)[:feature].astype(BF)
    for t in range(tile):
        dq_ref[t] = dq[:, t * nq:(t + 1) * nq]
        ho_ref[t] = dot(out_ref[t], w_ref[t], 0, 0).astype(BF)


def rest(ds, keys, out, w, feature):
    heads, latent, vd = w.shape
    rows, wide = keys.shape
    nq = out.shape[2]
    tile = TILE
    heads_of = lambda *shape: pl.BlockSpec((tile,) + shape, lambda i: (i, 0, 0))
    return pl.pallas_call(
        rest_kernel,
        grid=(heads // tile,),
        in_specs=[pl.BlockSpec((rows, tile * nq), lambda i: (0, i)),
                  pl.BlockSpec((rows, wide), lambda i: (0, 0)), heads_of(latent, nq),
                  heads_of(latent, vd)],
        out_specs=[heads_of(feature, nq), heads_of(nq, vd)],
        out_shape=[jax.ShapeDtypeStruct((heads, feature, nq), BF),
                   jax.ShapeDtypeStruct((heads, nq, vd), BF)],
        compiler_params=pltpu.CompilerParams(vmem_limit_bytes=REST_VMEM),
        cost_estimate=pl.CostEstimate(
            flops=1_000_000, bytes_accessed=100_000, transcendentals=0
        ),
    )(ds, keys, out, w)


def wanted_kernel(selected_ref, home_ref, out_ref):
    owners = out_ref.shape[0]
    blk_dev = home_ref.shape[0] * home_ref.shape[1] // owners
    names = selected_ref[...].T
    lane = lax.broadcasted_iota(jnp.int32, (names.shape[0], home_ref.shape[1]), 1)
    owner = lax.broadcasted_iota(jnp.int32, (owners, home_ref.shape[1]), 0)
    first = jnp.full(owner.shape, blk_dev, jnp.int32)
    last = jnp.full(owner.shape, -1, jnp.int32)
    for row in range(home_ref.shape[0]):
        named = jnp.zeros(lane.shape, jnp.int32)
        for k in range(names.shape[1]):
            named = jnp.where(names[:, k:k + 1] == lane + row * lane.shape[1], 1, named)
        named = jnp.max(named, axis=0, keepdims=True)
        home = home_ref[row:row + 1, :]
        here = (named > 0) & (lax.div(home, blk_dev) == owner)
        slot = lax.rem(home, blk_dev)
        first = jnp.minimum(first, jnp.where(here, slot, blk_dev))
        last = jnp.maximum(last, jnp.where(here, slot, -1))
    first = jnp.min(first, axis=1, keepdims=True)
    last = jnp.max(last, axis=1, keepdims=True)
    column = lax.broadcasted_iota(jnp.int32, out_ref.shape, 1)
    second = jnp.where(last > first, last, -1)
    out_ref[...] = jnp.where(column == 0, jnp.where(first < blk_dev, first, -1), second)


def wanted(selected_t, block_home, owners, blk_dev):
    vm = pl.BlockSpec(memory_space=pltpu.VMEM)
    return pl.pallas_call(
        wanted_kernel,
        in_specs=[vm, vm],
        out_specs=vm,
        out_shape=jax.ShapeDtypeStruct((owners, CAP), jnp.int32),
        cost_estimate=pl.CostEstimate(flops=3_000_000, bytes_accessed=10_000, transcendentals=0),
    )(selected_t, block_home.reshape(-1, 128))


def settle_kernel(asked_ref, returned_ref, out_ref, total):
    total[...] = jnp.zeros_like(total)

    def add(at, carry):
        slot = asked_ref[at]

        @pl.when(slot >= 0)
        def _():
            total[slot] += returned_ref[at].astype(F32)

        return carry

    lax.fori_loop(0, returned_ref.shape[0], add, 0)
    out_ref[...] = total[...].astype(BF)


def settle(asked, returned, blk_dev):
    _, share, feature = returned.shape
    return pl.pallas_call(
        settle_kernel,
        in_specs=[pl.BlockSpec(memory_space=pltpu.SMEM), pl.BlockSpec(memory_space=pltpu.VMEM)],
        out_specs=pl.BlockSpec(memory_space=pltpu.VMEM),
        out_shape=jax.ShapeDtypeStruct((blk_dev, share, feature), BF),
        scratch_shapes=[pltpu.VMEM((blk_dev, share, feature), F32)],
        cost_estimate=pl.CostEstimate(flops=500_000, bytes_accessed=1_000_000, transcendentals=0),
    )(asked, returned)


def by_ctx(move):
    return [(y * NZ + z, move(y) * NZ + z) for y in range(NY) for z in range(NZ)]


def to_z(k):
    return [(y * NZ + z, y * NZ + (z + k) % NZ) for y in range(NY) for z in range(NZ)]


def by_head(move):
    return [(x * NC + c, move(x, c)) for x in range(NX) for c in range(NC)]


def to_x(k):
    return by_head(lambda x, c: (x + k) % NX * NC + c)


def from_x(k):
    return by_head(lambda x, c: (x - k) % NX * NC + c)


OTHER_CORE = by_head(lambda x, c: x * NC + 1 - c)


def body(latent_cache, queries, selected, block_home, w_uv, out_grad):
    owners = NY * NZ
    blk_dev, block_len, feature = latent_cache.shape
    latent = w_uv.shape[1]
    total = block_home.shape[0]
    nq, heads, _ = queries.shape
    share = block_len // (NX * NC)
    head_at = lax.axis_index("head")
    ctx_at = lax.axis_index("ctx").astype(jnp.int32)

    flat = selected.reshape(-1)
    flat_home = jnp.sum(
        jnp.where(flat[:, None] == jnp.arange(total)[None, :], block_home[None, :], 0), axis=1
    )
    request = wanted(selected.T, block_home, owners, blk_dev)
    asked = lax.all_to_all(request, "ctx", split_axis=0, concat_axis=0, tiled=True)

    q_t = jnp.transpose(queries, (1, 2, 0))
    og_heads = jnp.swapaxes(out_grad, 0, 1)
    mine = lax.dynamic_slice_in_dim(latent_cache, head_at * share, share, axis=1)
    asked, og_heads, mine = lax.optimization_barrier((asked, og_heads, mine))
    asked = asked.reshape(-1)

    outgoing = mine[jnp.maximum(asked, 0)]
    arrived = lax.all_to_all(
        outgoing.reshape(owners, CAP, share, feature), "ctx", split_axis=0, concat_axis=0, tiled=True
    ).reshape(owners * CAP, share, feature)

    valid = (request >= 0).reshape(-1)
    count = jnp.arange(owners * CAP)
    place = jnp.sum((valid[None, :] & (count[None, :] < count[:, None])).astype(jnp.int32), axis=1)
    hit = valid[None, :] & (place[None, :] == jnp.arange(UNIQ)[:, None])
    source = jnp.sum(jnp.where(hit, count[None, :], 0), axis=1)
    slot_home = (jnp.arange(owners)[:, None] * blk_dev + jnp.maximum(request, 0)).reshape(-1)
    pool_home = jnp.sum(jnp.where(hit, slot_home[None, :], 0), axis=1)
    chosen = jnp.max(
        (flat_home.reshape(nq, -1)[:, :, None] == pool_home[None, None, :]).astype(jnp.int32), axis=1
    )
    spot = jnp.minimum(place, UNIQ - 1)

    bias = jnp.where(chosen > 0, 0.0, OUTSIDE).astype(BF).T
    d_latent = jnp.einsum(
        "hcv,hqv->hcq", w_uv, og_heads, preferred_element_type=F32
    ).astype(BF)
    arrived, bias, d_latent, source, spot = lax.optimization_barrier(
        (arrived, bias, d_latent, source, spot)
    )

    own = arrived[source].reshape(UNIQ * share, feature)
    parts = [own] + [lax.ppermute(own, "head", from_x(k)) for k in range(1, NX)]
    parts = parts + [lax.ppermute(part, "head", OTHER_CORE) for part in parts]

    ds, out, keys, own_a, next_a, send_a, own_b, next_b, send_b, near, *far = forward(
        jnp.stack([ctx_at // NZ, ctx_at % NZ]), parts, bias, q_t, d_latent, og_heads
    )

    flip, turn = by_ctx(lambda y: y ^ 1), by_ctx(lambda y: y ^ 3)
    got_a = lax.ppermute(send_a, "ctx", flip)
    got_b = lax.ppermute(send_b, "ctx", turn)

    far_in = [lax.ppermute(part, "head", OTHER_CORE) for part in far]
    size = UNIQ * share
    quarter = [near[k * size:(k + 1) * size] + far_in[k] for k in range(NX)]
    leaving = [part.astype(BF) for part in quarter[1:]]
    ahead = [lax.ppermute(part, "head", to_x(k + 1)) for k, part in enumerate(leaving)]

    ds, out, _, own_quarter = lax.optimization_barrier((ds, out, leaving, quarter[0]))
    d_query, out_heads = rest(ds, keys, out, w_uv, feature)
    ahead, got_a, got_b, d_query, out_heads = lax.optimization_barrier(
        (ahead, got_a, got_b, d_query, out_heads)
    )

    pass_a = (next_a + got_a[1].astype(F32)).astype(BF)
    pass_b = (next_b + got_b[1].astype(F32)).astype(BF)
    pass_a, pass_b = lax.optimization_barrier((pass_a, pass_b))
    last_a = lax.ppermute(pass_a, "ctx", turn)
    last_b = lax.ppermute(pass_b, "ctx", flip)

    ahead, own_quarter, out_heads, _, _ = lax.optimization_barrier(
        (ahead, own_quarter, out_heads, pass_a, pass_b)
    )
    summed = own_quarter
    for part in ahead:
        summed = summed + part.astype(F32)
    outbound = summed.astype(BF).reshape(UNIQ, share, feature)[spot]
    returned = lax.all_to_all(
        outbound.reshape(owners, CAP, share, feature), "ctx", split_axis=0, concat_axis=0, tiled=True
    ).reshape(owners * CAP, share, feature)

    head_out = with_layout_constraint(
        jnp.swapaxes(out_heads, 0, 1), Layout(major_to_minor=(0, 1, 2))
    )
    last_a, last_b, head_out, _ = lax.optimization_barrier((last_a, last_b, head_out, outbound))
    column = jnp.concatenate(
        [
            own_a + got_a[0].astype(F32) + last_a.astype(F32),
            own_b + got_b[0].astype(F32) + last_b.astype(F32),
        ],
        axis=1,
    )
    weight_sum = column[0]
    for k in (1, 6, 2, 5, 3, 4, 7):
        weight_sum = weight_sum + lax.ppermute(column[k].astype(BF), "ctx", to_z(k)).astype(F32)
    weight_grad = weight_sum.astype(BF)

    cache_grad = settle(asked, returned, blk_dev)
    return (
        head_out, jnp.transpose(d_query, (2, 0, 1)), cache_grad, weight_grad
    )


def solution(mesh):
    in_specs = (
        P("ctx", None, None),
        P("ctx", "head", None),
        P("ctx", None),
        P(),
        P("head", None, None),
        P("ctx", "head", None),
    )
    out_specs = (
        P("ctx", "head", None),
        P("ctx", "head", None),
        P("ctx", "head", None),
        P("head", "ctx", None),
    )
    return jax.shard_map(body, mesh=mesh, in_specs=in_specs, out_specs=out_specs, check_vma=False)
```

```python
import jax
import jax.numpy as jnp
from jax import lax
from jax.experimental import pallas as pl
from jax.experimental.layout import Layout, with_layout_constraint
from jax.experimental.pallas import tpu as pltpu
from jax.sharding import PartitionSpec as P

NY, NZ, NX, NC = 4, 8, 4, 2
UNIQ = 16
CAP = 2
OUTSIDE = -1.0e6
TILE = 4
SUB = 2
CHUNK = 256
POOL_COLS = 512
FORWARD_VMEM = 56 * 1024 * 1024
REST_VMEM = 56 * 1024 * 1024

softmax_scale = 192.0 ** (-0.5)
LOG2E = 1.4426950408889634

BF = jnp.bfloat16
F32 = jnp.float32


def dot(a, b, ca, cb):
    return lax.dot_general(a, b, (((ca,), (cb,)), ((), ())), preferred_element_type=F32)


def forward_kernel(
    at_ref, k0_ref, k1_ref, k2_ref, k3_ref, k4_ref, k5_ref, k6_ref, k7_ref, bias_ref, qt_ref,
    dlt_ref, og_ref, ds_ref, out_ref, keys_ref, own_a_ref, next_a_ref, send_a_ref,
    own_b_ref, next_b_ref, send_b_ref, near_ref, f0_ref, f1_ref, f2_ref, f3_ref,
    values_t, pieces, low_ref,
):
    step = pl.program_id(0)
    tile, nq, _ = og_ref.shape
    wide = keys_ref.shape[1]
    rows, feature = keys_ref.shape[0], k0_ref.shape[1]
    latent = dlt_ref.shape[1]
    part = k0_ref.shape[0]
    group = part // UNIQ
    half = pl.num_programs(0) // 2
    pool_refs = (near_ref, f0_ref, f1_ref, f2_ref, f3_ref)

    @pl.when(step == 0)
    def _():
        for at, ref in enumerate((k0_ref, k1_ref, k2_ref, k3_ref, k4_ref, k5_ref, k6_ref, k7_ref)):
            keys_ref[at * part:(at + 1) * part, :feature] = ref[...]
        owner = (lax.broadcasted_iota(jnp.int32, (rows, wide - feature), 0) // group) % UNIQ
        lane = lax.broadcasted_iota(jnp.int32, (rows, wide - feature), 1)
        keys_ref[:, feature:] = (owner == lane).astype(F32).astype(BF)
        values_t[...] = keys_ref[:, :latent].T
        for ref in pool_refs:
            ref[...] = jnp.zeros_like(ref)

    per = min(SUB, tile)
    sub = per * nq
    rest = jnp.zeros((wide - feature - UNIQ, sub), BF)
    bias = jnp.concatenate([bias_ref[...]] * per, axis=1)

    def scored(j):
        q = jnp.concatenate([qt_ref[j * per + t] for t in range(per)], axis=1)
        return jnp.concatenate([q, bias, rest], axis=0)

    def carried(j):
        return jnp.concatenate([dlt_ref[j * per + t] for t in range(per)], axis=1)

    cols = [slice(at, at + sub) for at in range(0, tile * nq, sub)]
    rate = softmax_scale * LOG2E
    outs, qs, dls = [], [], []
    chunks = [slice(k, k + CHUNK) for k in range(0, rows, CHUNK)]
    def top_of(s):
        t = s[0].max(axis=0, keepdims=True)
        for x in s[1:]:
            t = jnp.maximum(t, x.max(axis=0, keepdims=True))
        return t * rate
    n = len(cols)
    ss, dd, pp = [None] * n, [None] * n, [None] * n
    for j in range(n + 1):
        if j < n:
            ss[j], dd[j] = [], []
            q, dl = scored(j), carried(j)
            qs.append(q)
            dls.append(dl)
        if j > 0:
            pp[j - 1], total, inner = [], 0.0, 0.0
            top = top_of(ss[j - 1])
        for ki, k in enumerate(chunks):
            if j < n:
                ss[j].append(dot(keys_ref[k], q, 1, 0))
            if j > 0:
                p = jnp.exp2(ss[j - 1][ki] * rate - top)
                pp[j - 1].append(p)
                total = total + p.sum(axis=0, keepdims=True)
                inner = inner + (p * dd[j - 1][ki]).sum(axis=0, keepdims=True)
        if j > 0:
            inv = 1.0 / total
            inner = inner * inv
            scaled = inv * softmax_scale
        for ki, k in enumerate(chunks):
            if j < n:
                dd[j].append(dot(keys_ref[k, :latent], dl, 1, 0))
            if j > 0:
                p = pp[j - 1][ki]
                low_ref[k, cols[j - 1]] = (p * inv).astype(BF)
                ds_ref[k, cols[j - 1]] = (p * scaled * (dd[j - 1][ki] - inner)).astype(BF)
        if j > 0:
            out = dot(values_t[...], low_ref[:, cols[j - 1]], 1, 0).astype(BF)
            for t in range(per):
                out_ref[(j - 1) * per + t] = out[:, t * nq:(t + 1) * nq]
            outs.append(out)
    depth = min(POOL_COLS, tile * nq)
    for lo in range(0, tile * nq, depth):
        span = slice(lo, lo + depth)
        here = range(lo // sub, (lo + depth) // sub)
        q = jnp.concatenate([qs[j] for j in here], axis=1)
        dl = jnp.concatenate([dls[j] for j in here], axis=1)
        for k in chunks:
            main = dot(ds_ref[k, span], q[:latent], 1, 1) + dot(low_ref[k, span], dl, 1, 1)
            side = dot(ds_ref[k, span], q[latent:feature], 1, 1)
            at = k.start
            for ref in pool_refs:
                n = ref.shape[0]
                if 0 <= at < n:
                    m = min(n - at, k.stop - k.start)
                    ref[at:at + m, :latent] += main[:m]
                    ref[at:at + m, latent:] += side[:m]
                    main, side, at = main[m:], side[m:], at + m
                    if main.shape[0] == 0:
                        break
                at -= n
    y, z = at_ref[0], at_ref[1]
    for t in range(tile):
        at = t * nq % sub
        wt = dot(outs[t * nq // sub][:, at:at + nq], og_ref[t], 1, 0)
        wt = wt.reshape(NY, NZ, latent // (NY * NZ), wt.shape[1])
        for part_y in range(NY):
            for part_z in range(NZ):
                pieces[part_y ^ y, lax.rem(part_z - z + NZ, NZ), t] = wt[part_y, part_z]

    @pl.when(step < half)
    def _():
        own_a_ref[...] = pieces[0]
        next_a_ref[...] = pieces[3]
        send_a_ref[0] = pieces[1].astype(BF)
        send_a_ref[1] = pieces[2].astype(BF)

    @pl.when(step >= half)
    def _():
        own_b_ref[...] = pieces[0]
        next_b_ref[...] = pieces[1]
        send_b_ref[0] = pieces[3].astype(BF)
        send_b_ref[1] = pieces[2].astype(BF)


def forward(at, parts, bias, qt, dlt, og):
    heads, nq, vd = og.shape
    latent = dlt.shape[1]
    part, feature = parts[0].shape
    wide = (feature + UNIQ + 127) // 128 * 128
    rows = len(parts) * part
    tile = TILE
    steps = heads // tile
    per = steps // 2
    sub = latent // (NY * NZ)
    whole = lambda *shape: pl.BlockSpec(shape, lambda i: (0,) * len(shape))
    cols = lambda n: pl.BlockSpec((n, tile * nq), lambda i: (0, i))
    heads_of = lambda *shape: pl.BlockSpec((tile,) + shape, lambda i: (i, 0, 0))
    at_a = lambda i: jnp.minimum(i, per - 1)
    at_b = lambda i: jnp.maximum(i - per, 0)

    def pieces_at(at):
        one = pl.BlockSpec((NZ, tile, sub, vd), lambda i: (0, at(i), 0, 0))
        two = pl.BlockSpec((2, NZ, tile, sub, vd), lambda i: (0, 0, at(i), 0, 0))
        return [one, one, two]

    sizes = [rows // 2] + [part] * NX
    shape = jax.ShapeDtypeStruct
    piece_shapes = [
        shape((NZ, heads // 2, sub, vd), F32), shape((NZ, heads // 2, sub, vd), F32),
        shape((2, NZ, heads // 2, sub, vd), BF),
    ]
    return pl.pallas_call(
        forward_kernel,
        grid=(steps,),
        in_specs=[pl.BlockSpec(memory_space=pltpu.SMEM)]
        + [whole(part, feature)] * len(parts)
        + [whole(UNIQ, nq), heads_of(feature, nq), heads_of(latent, nq),
           heads_of(nq, vd)],
        out_specs=[cols(rows), heads_of(latent, nq), whole(rows, wide)]
        + pieces_at(at_a) + pieces_at(at_b) + [whole(n, feature) for n in sizes],
        out_shape=[
            shape((rows, heads * nq), BF),
            shape((heads, latent, nq), BF), shape((rows, wide), BF),
        ] + piece_shapes * 2 + [shape((n, feature), F32) for n in sizes],
        scratch_shapes=[
            pltpu.VMEM((latent, rows), BF), pltpu.VMEM((NY, NZ, tile, sub, vd), F32),
            pltpu.VMEM((rows, tile * nq), BF),
        ],
        compiler_params=pltpu.CompilerParams(vmem_limit_bytes=FORWARD_VMEM),
        cost_estimate=pl.CostEstimate(
            flops=4 * heads * nq * rows * (wide + 2 * latent), bytes_accessed=16_000_000,
            transcendentals=heads * nq * rows,
        ),
    )(at, *parts, bias, qt, dlt, og)


def rest_kernel(ds_ref, keys_ref, out_ref, w_ref, dq_ref, ho_ref):
    tile, feature, nq = dq_ref.shape
    dq = dot(keys_ref[...], ds_ref[...], 0, 0)[:feature].astype(BF)
    for t in range(tile):
        dq_ref[t] = dq[:, t * nq:(t + 1) * nq]
        ho_ref[t] = dot(out_ref[t], w_ref[t], 0, 0).astype(BF)


def rest(ds, keys, out, w, feature):
    heads, latent, vd = w.shape
    rows, wide = keys.shape
    nq = out.shape[2]
    tile = TILE
    heads_of = lambda *shape: pl.BlockSpec((tile,) + shape, lambda i: (i, 0, 0))
    return pl.pallas_call(
        rest_kernel,
        grid=(heads // tile,),
        in_specs=[pl.BlockSpec((rows, tile * nq), lambda i: (0, i)),
                  pl.BlockSpec((rows, wide), lambda i: (0, 0)), heads_of(latent, nq),
                  heads_of(latent, vd)],
        out_specs=[heads_of(feature, nq), heads_of(nq, vd)],
        out_shape=[jax.ShapeDtypeStruct((heads, feature, nq), BF),
                   jax.ShapeDtypeStruct((heads, nq, vd), BF)],
        compiler_params=pltpu.CompilerParams(vmem_limit_bytes=REST_VMEM),
        cost_estimate=pl.CostEstimate(
            flops=1_000_000, bytes_accessed=100_000, transcendentals=0
        ),
    )(ds, keys, out, w)


def wanted_kernel(selected_ref, home_ref, out_ref):
    owners = out_ref.shape[0]
    blk_dev = home_ref.shape[0] * home_ref.shape[1] // owners
    names = selected_ref[...].T
    lane = lax.broadcasted_iota(jnp.int32, (names.shape[0], home_ref.shape[1]), 1)
    owner = lax.broadcasted_iota(jnp.int32, (owners, home_ref.shape[1]), 0)
    first = jnp.full(owner.shape, blk_dev, jnp.int32)
    last = jnp.full(owner.shape, -1, jnp.int32)
    for row in range(home_ref.shape[0]):
        named = jnp.zeros(lane.shape, jnp.int32)
        for k in range(names.shape[1]):
            named = jnp.where(names[:, k:k + 1] == lane + row * lane.shape[1], 1, named)
        named = jnp.max(named, axis=0, keepdims=True)
        home = home_ref[row:row + 1, :]
        here = (named > 0) & (lax.div(home, blk_dev) == owner)
        slot = lax.rem(home, blk_dev)
        first = jnp.minimum(first, jnp.where(here, slot, blk_dev))
        last = jnp.maximum(last, jnp.where(here, slot, -1))
    first = jnp.min(first, axis=1, keepdims=True)
    last = jnp.max(last, axis=1, keepdims=True)
    column = lax.broadcasted_iota(jnp.int32, out_ref.shape, 1)
    second = jnp.where(last > first, last, -1)
    out_ref[...] = jnp.where(column == 0, jnp.where(first < blk_dev, first, -1), second)


def wanted(selected_t, block_home, owners, blk_dev):
    vm = pl.BlockSpec(memory_space=pltpu.VMEM)
    return pl.pallas_call(
        wanted_kernel,
        in_specs=[vm, vm],
        out_specs=vm,
        out_shape=jax.ShapeDtypeStruct((owners, CAP), jnp.int32),
        cost_estimate=pl.CostEstimate(flops=3_000_000, bytes_accessed=10_000, transcendentals=0),
    )(selected_t, block_home.reshape(-1, 128))


def settle_kernel(asked_ref, returned_ref, out_ref, total):
    total[...] = jnp.zeros_like(total)

    spare = out_ref.shape[0]

    def add(at, carry):
        slot = asked_ref[at]
        total[jnp.where(slot < 0, spare, slot)] += returned_ref[at].astype(F32)
        return carry

    lax.fori_loop(0, returned_ref.shape[0], add, 0, unroll=8)
    out_ref[...] = total[:spare].astype(BF)


def settle(asked, returned, blk_dev):
    _, share, feature = returned.shape
    return pl.pallas_call(
        settle_kernel,
        in_specs=[pl.BlockSpec(memory_space=pltpu.SMEM), pl.BlockSpec(memory_space=pltpu.VMEM)],
        out_specs=pl.BlockSpec(memory_space=pltpu.VMEM),
        out_shape=jax.ShapeDtypeStruct((blk_dev, share, feature), BF),
        scratch_shapes=[pltpu.VMEM((blk_dev + 1, share, feature), F32)],
        cost_estimate=pl.CostEstimate(flops=500_000, bytes_accessed=1_000_000, transcendentals=0),
    )(asked, returned)


def by_ctx(move):
    return [(y * NZ + z, move(y) * NZ + z) for y in range(NY) for z in range(NZ)]


def to_z(k):
    return [(y * NZ + z, y * NZ + (z + k) % NZ) for y in range(NY) for z in range(NZ)]


def by_head(move):
    return [(x * NC + c, move(x, c)) for x in range(NX) for c in range(NC)]


def to_x(k):
    return by_head(lambda x, c: (x + k) % NX * NC + c)


def from_x(k):
    return by_head(lambda x, c: (x - k) % NX * NC + c)


OTHER_CORE = by_head(lambda x, c: x * NC + 1 - c)


def body(latent_cache, queries, selected, block_home, w_uv, out_grad):
    owners = NY * NZ
    blk_dev, block_len, feature = latent_cache.shape
    latent = w_uv.shape[1]
    total = block_home.shape[0]
    nq, heads, _ = queries.shape
    share = block_len // (NX * NC)
    head_at = lax.axis_index("head")
    ctx_at = lax.axis_index("ctx").astype(jnp.int32)

    flat = selected.reshape(-1)
    flat_home = jnp.sum(
        jnp.where(flat[:, None] == jnp.arange(total)[None, :], block_home[None, :], 0), axis=1
    )
    request = wanted(selected.T, block_home, owners, blk_dev)
    asked = lax.all_to_all(request, "ctx", split_axis=0, concat_axis=0, tiled=True)

    q_t = jnp.transpose(queries, (1, 2, 0))
    og_heads = jnp.swapaxes(out_grad, 0, 1)
    mine = lax.dynamic_slice_in_dim(latent_cache, head_at * share, share, axis=1)
    asked, og_heads, mine = lax.optimization_barrier((asked, og_heads, mine))
    asked = asked.reshape(-1)

    outgoing = mine[jnp.maximum(asked, 0)]
    arrived = lax.all_to_all(
        outgoing.reshape(owners, CAP, share, feature), "ctx", split_axis=0, concat_axis=0, tiled=True
    ).reshape(owners * CAP, share, feature)

    valid = (request >= 0).reshape(-1)
    count = jnp.arange(owners * CAP)
    place = jnp.sum((valid[None, :] & (count[None, :] < count[:, None])).astype(jnp.int32), axis=1)
    hit = valid[None, :] & (place[None, :] == jnp.arange(UNIQ)[:, None])
    source = jnp.sum(jnp.where(hit, count[None, :], 0), axis=1)
    slot_home = (jnp.arange(owners)[:, None] * blk_dev + jnp.maximum(request, 0)).reshape(-1)
    pool_home = jnp.sum(jnp.where(hit, slot_home[None, :], 0), axis=1)
    chosen = jnp.max(
        (flat_home.reshape(nq, -1)[:, :, None] == pool_home[None, None, :]).astype(jnp.int32), axis=1
    )
    spot = jnp.minimum(place, UNIQ - 1)

    bias = jnp.where(chosen > 0, 0.0, OUTSIDE).astype(BF).T
    d_latent = jnp.einsum(
        "hcv,hqv->hcq", w_uv, og_heads, preferred_element_type=F32
    ).astype(BF)
    arrived, bias, d_latent, source, spot = lax.optimization_barrier(
        (arrived, bias, d_latent, source, spot)
    )

    own = arrived[source].reshape(UNIQ * share, feature)
    parts = [own] + [lax.ppermute(own, "head", from_x(k)) for k in range(1, NX)]
    parts = parts + [lax.ppermute(part, "head", OTHER_CORE) for part in parts]

    ds, out, keys, own_a, next_a, send_a, own_b, next_b, send_b, near, *far = forward(
        jnp.stack([ctx_at // NZ, ctx_at % NZ]), parts, bias, q_t, d_latent, og_heads
    )

    flip, turn = by_ctx(lambda y: y ^ 1), by_ctx(lambda y: y ^ 3)
    got_a = lax.ppermute(send_a, "ctx", flip)
    got_b = lax.ppermute(send_b, "ctx", turn)

    far_in = [lax.ppermute(part, "head", OTHER_CORE) for part in far]
    size = UNIQ * share
    quarter = [near[k * size:(k + 1) * size] + far_in[k] for k in range(NX)]
    leaving = [part.astype(BF) for part in quarter[1:]]
    ahead = [lax.ppermute(part, "head", to_x(k + 1)) for k, part in enumerate(leaving)]

    ds, out, _, own_quarter = lax.optimization_barrier((ds, out, leaving, quarter[0]))
    d_query, out_heads = rest(ds, keys, out, w_uv, feature)
    head_out = with_layout_constraint(
        jnp.swapaxes(out_heads, 0, 1), Layout(major_to_minor=(0, 1, 2))
    )
    ahead, got_a, got_b, d_query, head_out = lax.optimization_barrier(
        (ahead, got_a, got_b, d_query, head_out)
    )

    pass_a = (next_a + got_a[1].astype(F32)).astype(BF)
    pass_b = (next_b + got_b[1].astype(F32)).astype(BF)
    pass_a, pass_b = lax.optimization_barrier((pass_a, pass_b))
    last_a = lax.ppermute(pass_a, "ctx", turn)
    last_b = lax.ppermute(pass_b, "ctx", flip)

    ahead, own_quarter, _, _ = lax.optimization_barrier((ahead, own_quarter, pass_a, pass_b))
    summed = own_quarter
    for part in ahead:
        summed = summed + part.astype(F32)
    outbound = summed.astype(BF).reshape(UNIQ, share, feature)[spot]
    returned = lax.all_to_all(
        outbound.reshape(owners, CAP, share, feature), "ctx", split_axis=0, concat_axis=0, tiled=True
    ).reshape(owners * CAP, share, feature)

    last_a, last_b, _ = lax.optimization_barrier((last_a, last_b, outbound))
    column = jnp.concatenate(
        [
            own_a + got_a[0].astype(F32) + last_a.astype(F32),
            own_b + got_b[0].astype(F32) + last_b.astype(F32),
        ],
        axis=1,
    )
    down, up = column[4], column[3]
    for k in (5, 6, 7, 0):
        down = lax.ppermute(down.astype(BF), "ctx", to_z(NZ - 1)).astype(F32)
        if k:
            down = down + column[k]
    for k in (2, 1, 0):
        up = lax.ppermute(up.astype(BF), "ctx", to_z(1)).astype(F32)
        if k:
            up = up + column[k]
    weight_sum = column[0] + down + up
    weight_grad = weight_sum.astype(BF)

    cache_grad = settle(asked, returned, blk_dev)
    return (
        head_out, jnp.transpose(d_query, (2, 0, 1)), cache_grad, weight_grad
    )


def solution(mesh):
    in_specs = (
        P("ctx", None, None),
        P("ctx", "head", None),
        P("ctx", None),
        P(),
        P("head", None, None),
        P("ctx", "head", None),
    )
    out_specs = (
        P("ctx", "head", None),
        P("ctx", "head", None),
        P("ctx", "head", None),
        P("head", "ctx", None),
    )
    return jax.shard_map(body, mesh=mesh, in_specs=in_specs, out_specs=out_specs, check_vma=False)
```
